512 devices in a mesh: bn: 32 (over x, y), grp: 16 (over z, core).
Axes of the slice: x: 4, y: 8, z: 8, core: 2. Of those that a mesh axis runs over, the one named last changes fastest.
Arguments:
- block_input: bfloat16 [16, 32, 29, 29, 176], P('grp', 'bn'), may hold values from -180 to 180
- cotangent: bfloat16 [16, 32, 29, 29, 176], P('grp', 'bn'), may hold values from -70 to 70
- w_expand: bfloat16 [176, 1056], replicated, may hold values from -0.4375 to 0.4375
- gain_expand: float32 [1056], replicated, may hold values from 0.1 to 1.9
- shift_expand: float32 [1056], replicated, may hold values from -3 to 3
- w_depth: bfloat16 [25, 1056], replicated, may hold values from -1.25 to 1.25
- gain_depth: float32 [1056], replicated, may hold values from 0.1 to 1.9
- shift_depth: float32 [1056], replicated, may hold values from -3 to 3
- w_reduce: bfloat16 [1056, 44], replicated, may hold values from -0.1875 to 0.1875
- b_reduce: float32 [44], replicated, may hold values from -4 to 4
- w_restore: bfloat16 [44, 1056], replicated, may hold values from -0.875 to 0.875
- b_restore: float32 [1056], replicated, may hold values from -4 to 4
- w_project: bfloat16 [1056, 176], replicated, may hold values from -0.1875 to 0.1875
- gain_project: float32 [176], replicated, may hold values from 0.1 to 1.9
- upper_grads: float32 [512, 131072], P(('bn', 'grp')), may hold values from -1 to 1
Outputs:
- input_grad: bfloat16 [16, 32, 29, 29, 176], P('grp', 'bn')
- grad_expand: float32 [176, 1056], replicated
- grad_gain_expand: float32 [1056], replicated
- grad_shift_expand: float32 [1056], replicated
- grad_depth: float32 [25, 1056], replicated
- grad_gain_depth: float32 [1056], replicated
- grad_shift_depth: float32 [1056], replicated
- grad_reduce: float32 [1056, 44], replicated
- grad_b_reduce: float32 [44], replicated
- grad_restore: float32 [44, 1056], replicated
- grad_b_restore: float32 [1056], replicated
- grad_project: float32 [1056, 176], replicated
- grad_gain_project: float32 [176], replicated
- upper_summed: float32 [131072], replicated
The draws below stay inside these ranges and needn't reach their ends.
All inputs are finite; a program needn't handle non-finite values.
Results may differ from the reference program's by a relative error of at most 0.0054.
Values sent between devices are 32-bit elements; how exact they have to be, the bound alone decides.
No kernel may reach another device: no remote copies, remote signals or barrier semaphores. Data moves between devices by JAX's collectives and lax.ppermute only.
A program may use at most 64 MiB of HBM per device.

```python
import math
import jax
import jax.numpy as jnp
from jax import lax

C = 176
HID = 1056
SE = 44
KER = 5
SIDE = 29
BUCKET = 131072
GROUPS = 16
GROUP_IMGS = 32
WORKERS = 512
IMAGES = 512


def ramp_values(key, full_shape, base, channel_top, noise_draw):
    offset_key, channel_key = jax.random.split(key, 2)
    offset = jax.random.uniform(offset_key, (full_shape[-1],), jnp.float32, -0.5, 0.5)
    channel = jnp.exp(jax.random.uniform(channel_key, (full_shape[-1],), jnp.float32, 0.0, math.log(channel_top)))
    position = jnp.arange(full_shape[1], dtype=jnp.float32) / max(full_shape[1] - 1, 1)
    rising = jnp.power(base, position)
    return (noise_draw + offset) * channel * rising[None, :, None, None, None]


def draw_block_input(key, part):
    key = jax.random.fold_in(key, 11)
    noise_key = jax.random.fold_in(key, 0)
    rest_key = jax.random.fold_in(key, 2)
    full_shape = (GROUPS, GROUP_IMGS, SIDE, SIDE, C)
    noise_draw = jnp.clip(jax.random.normal(noise_key, full_shape, jnp.float32), -5.0, 5.0)
    return ramp_values(rest_key, full_shape, 4.0, 4.0, noise_draw).astype(jnp.bfloat16)


def draw_cotangent(key, part):
    key = jax.random.fold_in(key, 12)
    noise_key = jax.random.fold_in(key, 0)
    rest_key = jax.random.fold_in(key, 2)
    full_shape = (GROUPS, GROUP_IMGS, SIDE, SIDE, C)
    noise_draw = jnp.clip(jax.random.normal(noise_key, full_shape, jnp.float32), -5.0, 5.0)
    return ramp_values(rest_key, full_shape, 3.0, 2.0, noise_draw).astype(jnp.bfloat16)


def raised(array, rng, source, target, shards_of, factor):
    def block_of(axis_at):
        return (jnp.arange(array.shape[axis_at]) // (array.shape[axis_at] // shards_of)).reshape((-1,) + (1,) * (array.ndim - 1 - axis_at))

    one_side = jax.random.permutation(rng, shards_of)[block_of(target)]
    far = (block_of(target) + shards_of // 2) % shards_of
    return jnp.where((block_of(source) == one_side) | (block_of(source) == far), factor * array, array)


def shard_levels(key, shape, shards, smallest, top_value):
    factor_of, own = 1.0, jax.random.fold_in(key, 6)
    for dim, parts in shards:
        steps = jnp.exp(jax.random.uniform(jax.random.fold_in(own, dim), (parts,), jnp.float32, smallest / len(shards), top_value / len(shards)))
        factor_of = factor_of * jnp.repeat(steps, shape[dim] // parts).reshape([-1 if axis == dim else 1 for axis in range(len(shape))])
    return factor_of


def normal_values(rng, shape, deviation, limit, cuts=(), kind=jnp.bfloat16):
    drawn = jax.random.normal(rng, shape, jnp.float32) * deviation
    if len(cuts) > 0:
        drawn = shard_levels(rng, shape, cuts, -0.22, 0.18) * drawn
    return jnp.clip(drawn, min=-limit, max=limit).astype(kind)


def bell_draw_with(stream_key, dims, scale, most, pieces, heavy, held_as=jnp.bfloat16):
    result = scale * jax.random.normal(stream_key, dims, jnp.float32)
    if pieces:
        result = result * shard_levels(stream_key, dims, pieces, -0.22, 0.18)
    return jnp.clip(raised(result, jax.random.fold_in(stream_key, 3), *heavy), -most, most).astype(held_as)


def setup_inputs(seed: int = 0) -> dict:
    key_of = jax.random.split(jax.random.key(seed), 16)
    return {
        "block_input": draw_block_input(jax.random.fold_in(key_of[15], 71), 0),
        "cotangent": draw_cotangent(jax.random.fold_in(key_of[15], 71), 0),
        "w_expand": normal_values(key_of[2], (C, HID), C ** -0.5, 0.4375),
        "gain_expand": jnp.clip(1.0 + 0.18 * jax.random.normal(key_of[3], (HID,), jnp.float32), 0.1, 1.9),
        "shift_expand": normal_values(key_of[4], (HID,), 0.5, 3.0, (), jnp.float32),
        "w_depth": normal_values(key_of[5], (KER * KER, HID), (KER * KER) ** -0.5, 1.25),
        "gain_depth": jnp.clip(1.0 + 0.18 * jax.random.normal(key_of[6], (HID,), jnp.float32), 0.1, 1.9),
        "shift_depth": normal_values(key_of[7], (HID,), 0.5, 3.0, (), jnp.float32),
        "w_reduce": normal_values(key_of[8], (HID, SE), HID ** -0.5, 0.1875),
        "b_reduce": normal_values(key_of[9], (SE,), 1.0, 4.0, (), jnp.float32),
        "w_restore": normal_values(key_of[10], (SE, HID), SE ** -0.5, 0.875),
        "b_restore": normal_values(key_of[11], (HID,), 1.0, 4.0, (), jnp.float32),
        "w_project": normal_values(key_of[12], (HID, C), HID ** -0.5, 0.1875),
        "gain_project": jnp.clip(1.0 + 0.18 * jax.random.normal(key_of[13], (C,), jnp.float32), 0.1, 1.9),
        "upper_grads": bell_draw_with(key_of[14], (WORKERS, BUCKET), WORKERS ** -0.5, 1.0, ((0, 512),), (0, 1, 512, 6.0), jnp.float32),
    }


EPSILON = 0.001
exact_precision = lax.Precision.HIGHEST

def silu_slope(values):
    logistic = jax.nn.sigmoid(values)
    return logistic * (1.0 + values * (1.0 - logistic))

def pad_map(field):
    margin = KER // 2
    return jnp.pad(field, ((0, 0), (margin, margin), (margin, margin), (0, 0)))

def depthwise(field, kernel):
    extent = field.shape[1]
    padded = pad_map(field)
    summed = jnp.zeros(field.shape, jnp.float32)
    for row_off in range(KER):
        for col_off in range(KER):
            window = padded[:, row_off:row_off + extent, col_off:col_off + extent, :].astype(jnp.float32)
            summed = summed + window * kernel[row_off * KER + col_off].astype(jnp.float32)
    return summed

def depth_input_grad(grad_out, kernel):
    extent = grad_out.shape[1]
    margin = KER // 2
    padded = pad_map(grad_out)
    summed = jnp.zeros(grad_out.shape, jnp.float32)
    for row_off in range(KER):
        for col_off in range(KER):
            row_start = 2 * margin - row_off
            col_start = 2 * margin - col_off
            window = padded[:, row_start:row_start + extent, col_start:col_start + extent, :]
            summed = summed + window * kernel[row_off * KER + col_off].astype(jnp.float32)
    return summed

def depth_kernel_grad(field, grad_out):
    extent = field.shape[1]
    padded = pad_map(field)
    columns = []
    for row_off in range(KER):
        for col_off in range(KER):
            window = padded[:, row_off:row_off + extent, col_off:col_off + extent, :].astype(jnp.float32)
            columns.append(lax.optimization_barrier(jnp.sum(window * grad_out, axis=(0, 1, 2))))
    return jnp.stack(columns)

def group_norm(values):
    center = lax.optimization_barrier(jnp.mean(values, axis=(0, 1, 2)))
    spread = lax.optimization_barrier(jnp.mean(jnp.square(values - center), axis=(0, 1, 2)))
    scaling = lax.rsqrt(spread + EPSILON)
    return ((values - center) * scaling, scaling)

def norm_back(grad_normed, normed, scaling):
    first = lax.optimization_barrier(jnp.mean(grad_normed, axis=(0, 1, 2)))
    second = lax.optimization_barrier(jnp.mean(grad_normed * normed, axis=(0, 1, 2)))
    return scaling * (grad_normed - first - normed * second)

def group_pass(images, cot_group, params):
    w_expand, gain_expand, shift_expand, w_depth, gain_depth, shift_depth, w_reduce, b_reduce, w_restore, b_restore, w_project, gain_project = params
    incoming = cot_group.astype(jnp.float32)
    extent = images.shape[1]
    pre_expand = jnp.dot(images, w_expand, preferred_element_type=jnp.float32)
    normed_one, scale_one = group_norm(pre_expand)
    act_one = normed_one * gain_expand + shift_expand
    expanded = jax.nn.silu(act_one).astype(jnp.bfloat16)
    pre_depth = depthwise(expanded, w_depth)
    normed_two, scale_two = group_norm(pre_depth)
    act_two = normed_two * gain_depth + shift_depth
    activated = jax.nn.silu(act_two).astype(jnp.bfloat16)
    pooled = lax.optimization_barrier(jnp.mean(activated.astype(jnp.float32), axis=(1, 2)))
    logit_reduce = jnp.dot(pooled, w_reduce.astype(jnp.float32), precision=exact_precision) + b_reduce
    squeezed = jax.nn.silu(logit_reduce)
    logit_restore = jnp.dot(squeezed, w_restore.astype(jnp.float32), precision=exact_precision) + b_restore
    excite = jax.nn.sigmoid(logit_restore)
    hidden = (activated.astype(jnp.float32) * excite[:, None, None, :]).astype(jnp.bfloat16)
    pre_project = jnp.dot(hidden, w_project, preferred_element_type=jnp.float32)
    normed_three, scale_three = group_norm(pre_project)
    grad_gain_project = lax.optimization_barrier(jnp.sum(incoming * normed_three, axis=(0, 1, 2)))
    grad_pre_project = norm_back(incoming * gain_project, normed_three, scale_three).astype(jnp.bfloat16)
    grad_project = jnp.dot(hidden.reshape(-1, hidden.shape[-1]).T, grad_pre_project.reshape(-1, grad_pre_project.shape[-1]), preferred_element_type=jnp.float32)
    grad_hidden = jnp.dot(grad_pre_project, w_project.T, preferred_element_type=jnp.float32)
    grad_excite = lax.optimization_barrier(jnp.sum(grad_hidden * activated.astype(jnp.float32), axis=(1, 2)))
    grad_logit_restore = grad_excite * excite * (1.0 - excite)
    grad_restore = jnp.dot(squeezed.T, grad_logit_restore, precision=exact_precision)
    grad_b_restore = lax.optimization_barrier(jnp.sum(grad_logit_restore, axis=0))
    grad_squeezed = jnp.dot(grad_logit_restore, w_restore.astype(jnp.float32).T, precision=exact_precision)
    grad_logit_reduce = grad_squeezed * silu_slope(logit_reduce)
    grad_reduce = jnp.dot(pooled.T, grad_logit_reduce, precision=exact_precision)
    grad_b_reduce = lax.optimization_barrier(jnp.sum(grad_logit_reduce, axis=0))
    grad_pooled = jnp.dot(grad_logit_reduce, w_reduce.astype(jnp.float32).T, precision=exact_precision)
    grad_activated = grad_hidden * excite[:, None, None, :] + grad_pooled[:, None, None, :] / (extent * extent)
    grad_act_two = grad_activated * silu_slope(act_two)
    grad_shift_depth = lax.optimization_barrier(jnp.sum(grad_act_two, axis=(0, 1, 2)))
    grad_gain_depth = lax.optimization_barrier(jnp.sum(grad_act_two * normed_two, axis=(0, 1, 2)))
    grad_pre_depth = norm_back(grad_act_two * gain_depth, normed_two, scale_two)
    grad_depth = depth_kernel_grad(expanded, grad_pre_depth)
    grad_expanded = depth_input_grad(grad_pre_depth, w_depth)
    grad_act_one = grad_expanded * silu_slope(act_one)
    grad_shift_expand = lax.optimization_barrier(jnp.sum(grad_act_one, axis=(0, 1, 2)))
    grad_gain_expand = lax.optimization_barrier(jnp.sum(grad_act_one * normed_one, axis=(0, 1, 2)))
    grad_pre_expand = norm_back(grad_act_one * gain_expand, normed_one, scale_one).astype(jnp.bfloat16)
    grad_expand = jnp.dot(images.reshape(-1, images.shape[-1]).T, grad_pre_expand.reshape(-1, grad_pre_expand.shape[-1]), preferred_element_type=jnp.float32)
    input_grad = (incoming + jnp.dot(grad_pre_expand, w_expand.T, preferred_element_type=jnp.float32)).astype(jnp.bfloat16)
    window_grads = (grad_expand, grad_gain_expand, grad_shift_expand, grad_depth, grad_gain_depth, grad_shift_depth, grad_reduce, grad_b_reduce, grad_restore, grad_b_restore, grad_project, grad_gain_project)
    return (input_grad, window_grads)

def reference(block_input, cotangent, w_expand, gain_expand, shift_expand, w_depth, gain_depth, shift_depth, w_reduce, b_reduce, w_restore, b_restore, w_project, gain_project, upper_grads):
    params = (w_expand, gain_expand, shift_expand, w_depth, gain_depth, shift_depth, w_reduce, b_reduce, w_restore, b_restore, w_project, gain_project)

    def one_group(paired):
        return group_pass(paired[0], paired[1], params)
    input_grad, stacked = lax.map(one_group, (block_input, cotangent))
    scaled = [lax.optimization_barrier(jnp.sum(piece, axis=0)) / IMAGES for piece in stacked]
    upper_summed = lax.optimization_barrier(jnp.sum(upper_grads, axis=0))
    return (input_grad, scaled[0], scaled[1], scaled[2], scaled[3], scaled[4], scaled[5], scaled[6], scaled[7], scaled[8], scaled[9], scaled[10], scaled[11], upper_summed)
```

```python
import jax
import jax.numpy as jnp
from jax import lax
from jax.sharding import Mesh, PartitionSpec as P

KER = 5


EPSILON = 0.001
exact_precision = lax.Precision.HIGHEST


def silu_slope(values):
    logistic = jax.nn.sigmoid(values)
    return logistic * (1.0 + values * (1.0 - logistic))


def pad_map(field):
    margin = KER // 2
    return jnp.pad(field, ((0, 0), (margin, margin), (margin, margin), (0, 0)))


def depthwise(field, kernel):
    extent = field.shape[1]
    padded = pad_map(field)
    summed = jnp.zeros(field.shape, jnp.float32)
    for row_off in range(KER):
        for col_off in range(KER):
            window = padded[:, row_off : row_off + extent, col_off : col_off + extent, :].astype(
                jnp.float32
            )
            summed = summed + window * kernel[row_off * KER + col_off].astype(jnp.float32)
    return summed


def depth_input_grad(grad_out, kernel):
    extent = grad_out.shape[1]
    margin = KER // 2
    padded = pad_map(grad_out)
    summed = jnp.zeros(grad_out.shape, jnp.float32)
    for row_off in range(KER):
        for col_off in range(KER):
            row_start = 2 * margin - row_off
            col_start = 2 * margin - col_off
            window = padded[:, row_start : row_start + extent, col_start : col_start + extent, :]
            summed = summed + window * kernel[row_off * KER + col_off].astype(jnp.float32)
    return summed


def depth_kernel_grad(field, grad_out):
    extent = field.shape[1]
    padded = pad_map(field)
    columns = []
    for row_off in range(KER):
        for col_off in range(KER):
            window = padded[:, row_off : row_off + extent, col_off : col_off + extent, :].astype(
                jnp.float32
            )
            columns.append(jnp.sum(window * grad_out, axis=(0, 1, 2)))
    return jnp.stack(columns)


AXES = ("x", "y", "z", "core")
GROUP = ("x", "y")


def group_rows(values):
    return values.shape[0] * values.shape[1] * values.shape[2] * lax.axis_size(GROUP)


def local_moments(values):
    mean = jnp.mean(values, axis=(0, 1, 2))
    spread = jnp.mean(jnp.square(values - mean), axis=(0, 1, 2))
    return mean, spread


def merge_moments(means, spreads):
    center = jnp.mean(means, axis=0)
    return center, jnp.mean(spreads + jnp.square(means - center), axis=0)


def gather_by_exchange(vector):
    size = lax.axis_size(GROUP)
    tiled = jnp.broadcast_to(vector[None], (size,) + vector.shape)
    return lax.all_to_all(tiled, GROUP, 0, 0, tiled=True)


def ring_parts(vector, axis):
    size = lax.axis_size(axis)
    return [vector] + [
        lax.ppermute(vector, axis, [(i, (i + step) % size) for i in range(size)])
        for step in range(1, size)
    ]


def doubling_sum(vector):
    for axis in GROUP:
        size = lax.axis_size(axis)
        step = 1
        while step < size:
            vector = vector + lax.ppermute(vector, axis, [(i, i ^ step) for i in range(size)])
            step *= 2
    return vector


def rows_to_norm(values, center, spread):
    scaling = lax.rsqrt(spread + EPSILON)
    return ((values - center) * scaling, scaling)


def per_device(
    block_input,
    cotangent,
    w_expand,
    gain_expand,
    shift_expand,
    w_depth,
    gain_depth,
    shift_depth,
    w_reduce,
    b_reduce,
    w_restore,
    b_restore,
    w_project,
    gain_project,
    upper_grads,
):
    upper_summed = lax.psum(upper_grads[0], AXES)
    images = block_input[0]
    incoming = cotangent[0].astype(jnp.float32)
    extent = images.shape[1]
    pre_expand = jnp.dot(images, w_expand, preferred_element_type=jnp.float32)
    hid = pre_expand.shape[-1]
    gathered = gather_by_exchange(jnp.stack(local_moments(pre_expand)))
    center_one, spread_one = merge_moments(gathered[:, 0], gathered[:, 1])
    normed_one, scale_one = rows_to_norm(pre_expand, center_one, spread_one)
    act_one = normed_one * gain_expand + shift_expand
    expanded = jax.nn.silu(act_one).astype(jnp.bfloat16)
    pre_depth = depthwise(expanded, w_depth)
    gathered = lax.all_gather(jnp.concatenate(local_moments(pre_depth)), GROUP)
    center_two, spread_two = merge_moments(gathered[:, :hid], gathered[:, hid:])
    normed_two, scale_two = rows_to_norm(pre_depth, center_two, spread_two)
    act_two = normed_two * gain_depth + shift_depth
    activated = jax.nn.silu(act_two).astype(jnp.bfloat16)
    pooled = jnp.mean(activated.astype(jnp.float32), axis=(1, 2))
    logit_reduce = (
        jnp.dot(pooled, w_reduce.astype(jnp.float32), precision=exact_precision) + b_reduce
    )
    squeezed = jax.nn.silu(logit_reduce)
    logit_restore = (
        jnp.dot(squeezed, w_restore.astype(jnp.float32), precision=exact_precision) + b_restore
    )
    excite = jax.nn.sigmoid(logit_restore)
    hidden = (activated.astype(jnp.float32) * excite[:, None, None, :]).astype(jnp.bfloat16)
    pre_project = jnp.dot(hidden, w_project, preferred_element_type=jnp.float32)
    row_count = group_rows(pre_project)
    mean_three, spread_three = local_moments(pre_project)
    cot_sum = jnp.sum(incoming, axis=(0, 1, 2))
    cot_dev = jnp.sum(incoming * (pre_project - mean_three), axis=(0, 1, 2))
    packed = jnp.stack([mean_three, spread_three, cot_sum, cot_dev])
    for axis in GROUP:
        parts = jnp.stack(ring_parts(packed, axis))
        center, spread = merge_moments(parts[:, 0], parts[:, 1])
        dev = jnp.sum(parts[:, 3] + parts[:, 2] * (parts[:, 0] - center), axis=0)
        packed = jnp.stack([center, spread, jnp.sum(parts[:, 2], axis=0), dev])
    normed_three, scale_three = rows_to_norm(pre_project, packed[0], packed[1])
    second = packed[3] * scale_three
    grad_gain_project = jnp.sum(incoming * normed_three, axis=(0, 1, 2))
    grad_pre_project = (
        scale_three
        * gain_project
        * (incoming - packed[2] / row_count - normed_three * (second / row_count))
    ).astype(jnp.bfloat16)
    grad_project = jnp.dot(
        hidden.reshape(-1, hidden.shape[-1]).T,
        grad_pre_project.reshape(-1, grad_pre_project.shape[-1]),
        preferred_element_type=jnp.float32,
    )
    grad_hidden = jnp.dot(grad_pre_project, w_project.T, preferred_element_type=jnp.float32)
    grad_excite = jnp.sum(grad_hidden * activated.astype(jnp.float32), axis=(1, 2))
    grad_logit_restore = grad_excite * excite * (1.0 - excite)
    grad_restore = jnp.dot(squeezed.T, grad_logit_restore, precision=exact_precision)
    grad_b_restore = jnp.sum(grad_logit_restore, axis=0)
    grad_squeezed = jnp.dot(
        grad_logit_restore, w_restore.astype(jnp.float32).T, precision=exact_precision
    )
    grad_logit_reduce = grad_squeezed * silu_slope(logit_reduce)
    grad_reduce = jnp.dot(pooled.T, grad_logit_reduce, precision=exact_precision)
    grad_b_reduce = jnp.sum(grad_logit_reduce, axis=0)
    grad_pooled = jnp.dot(
        grad_logit_reduce, w_reduce.astype(jnp.float32).T, precision=exact_precision
    )
    grad_activated = grad_hidden * excite[:, None, None, :] + grad_pooled[:, None, None, :] / (
        extent * extent
    )
    grad_act_two = grad_activated * silu_slope(act_two)
    grad_shift_depth = jnp.sum(grad_act_two, axis=(0, 1, 2))
    grad_gain_depth = jnp.sum(grad_act_two * normed_two, axis=(0, 1, 2))
    sums = doubling_sum(jnp.concatenate([grad_shift_depth, grad_gain_depth]))
    grad_pre_depth = (scale_two * gain_depth) * (
        grad_act_two - sums[:hid] / row_count - normed_two * (sums[hid:] / row_count)
    )
    grad_depth = depth_kernel_grad(expanded, grad_pre_depth)
    grad_expanded = depth_input_grad(grad_pre_depth, w_depth)
    grad_act_one = grad_expanded * silu_slope(act_one)
    grad_shift_expand = jnp.sum(grad_act_one, axis=(0, 1, 2))
    grad_gain_expand = jnp.sum(grad_act_one * normed_one, axis=(0, 1, 2))
    sums = jnp.concatenate([grad_shift_expand, grad_gain_expand])
    for axis in GROUP:
        sums = lax.psum(sums, axis)
    grad_pre_expand = (
        (scale_one * gain_expand)
        * (grad_act_one - sums[:hid] / row_count - normed_one * (sums[hid:] / row_count))
    ).astype(jnp.bfloat16)
    grad_expand = jnp.dot(
        images.reshape(-1, images.shape[-1]).T,
        grad_pre_expand.reshape(-1, grad_pre_expand.shape[-1]),
        preferred_element_type=jnp.float32,
    )
    input_grad = (
        incoming + jnp.dot(grad_pre_expand, w_expand.T, preferred_element_type=jnp.float32)
    ).astype(jnp.bfloat16)
    pieces = (
        grad_expand,
        grad_gain_expand,
        grad_shift_expand,
        grad_depth,
        grad_gain_depth,
        grad_shift_depth,
        grad_reduce,
        grad_b_reduce,
        grad_restore,
        grad_b_restore,
        grad_project,
        grad_gain_project,
    )
    flat = jnp.concatenate([piece.reshape(-1) for piece in pieces])
    flat, upper_summed = lax.optimization_barrier((flat, upper_summed))
    flat = lax.psum(flat, AXES)
    images_total = images.shape[0] * lax.axis_size(AXES)
    flat = flat / images_total
    scaled = []
    start = 0
    for piece in pieces:
        scaled.append(flat[start : start + piece.size].reshape(piece.shape))
        start += piece.size
    return (
        input_grad[None],
        scaled[0],
        scaled[1],
        scaled[2],
        scaled[3],
        scaled[4],
        scaled[5],
        scaled[6],
        scaled[7],
        scaled[8],
        scaled[9],
        scaled[10],
        scaled[11],
        upper_summed,
    )


def solution(mesh):
    chips = Mesh(mesh.devices.reshape(4, 8, 8, 2), AXES)
    return jax.shard_map(
        per_device,
        mesh=chips,
        in_specs=(
            P(("z", "core"), GROUP, None, None, None),
            P(("z", "core"), GROUP, None, None, None),
            P(),
            P(),
            P(),
            P(),
            P(),
            P(),
            P(),
            P(),
            P(),
            P(),
            P(),
            P(),
            P(AXES, None),
        ),
        out_specs=(
            P(("z", "core"), GROUP, None, None, None),
            P(),
            P(),
            P(),
            P(),
            P(),
            P(),
            P(),
            P(),
            P(),
            P(),
            P(),
            P(),
            P(),
        ),
        check_vma=False,
    )
```

```python
import functools

import jax
import jax.numpy as jnp
from jax import lax
from jax.experimental import pallas as pl
from jax.experimental.pallas import tpu as pltpu
from jax.sharding import Mesh, PartitionSpec as P

KER = 5
EPSILON = 0.001
SHAPE = (4, 8, 8, 2)
AXES = ("x", "y", "z", "core")
GROUP = ("x", "y")
PLANE = ("x", "y", "core")
SIDE = 29
WIDE = 32
ROWS = SIDE * WIDE
HALO = (SIDE + KER - 1) * WIDE
C = 176
HID = 1056
LANES = 128
CHUNKS = 9
PADDED = CHUNKS * LANES
SE = 44
SE_ROWS = 48
SPOTS = SIDE * SIDE
GAIN_ONE, SHIFT_ONE, GAIN_TWO, SHIFT_TWO, BIAS = 25, 26, 27, 28, 29
TABLE = 32
EARLY = C + 2 * SE_ROWS
EARLY_ROWS = 2560
LATE = C + TABLE
LATE_ROWS = 2048
F32 = jnp.float32
BF16 = jnp.bfloat16


def dot(left, right, left_dim=1, right_dim=0):
    return lax.dot_general(
        left, right, (((left_dim,), (right_dim,)), ((), ())), preferred_element_type=F32
    )


def logistic(values):
    return 0.5 + 0.5 * jnp.tanh(0.5 * values)


def valid_mask(lanes=LANES):
    return lax.broadcasted_iota(jnp.int32, (WIDE, lanes), 0) < SIDE


def row_at(index):
    return pl.ds(pl.multiple_of(index * WIDE, WIDE), WIDE)


def each_row(body, init, unroll=1):
    return lax.fori_loop(0, SIDE, body, init, unroll=unroll)


def col_sum(values):
    return jnp.sum(values, axis=0, keepdims=True)


def zeros(lanes=LANES):
    return jnp.zeros((WIDE, lanes), F32)


def share(pair, ref):
    ref[...] = jnp.broadcast_to(pair[None], ref.shape)


def pair_rows(first, second):
    return jnp.where(lax.broadcasted_iota(jnp.int32, (2, first.shape[1]), 0) == 0, first, second)


def spread_of(ref, mean, mask):
    def body(i, acc):
        dev = jnp.where(mask, ref[row_at(i), :] - mean, 0.0)
        return acc + dev * dev

    return col_sum(each_row(body, zeros(mean.shape[1]))) / SPOTS


def merged(gathered):
    peers = gathered.shape[0]
    total = jnp.sum(gathered, axis=0)
    center = total[0:1] / peers
    dev = jnp.sum(jnp.square(gathered[:, 0:1, :] - center[None]), axis=0)
    spread = (total[1:2] + dev) / peers
    return center, lax.rsqrt(spread + EPSILON)


def widen(map_ref, flat_ref, line_ref):
    line_ref[...] = jnp.zeros_like(line_ref)
    for i in range(SIDE):
        line_ref[i % 2, 0:SIDE, :] = map_ref[i].astype(F32)
        flat_ref[i * WIDE : (i + 1) * WIDE, :] = line_ref[i % 2].astype(BF16)


def stats_kernel(x_ref, w_ref, xpad_ref, stat_ref, pre_ref, line_ref):
    @pl.when(pl.program_id(0) == 0)
    def _():
        widen(x_ref, xpad_ref, line_ref)

    pre_ref[...] = dot(xpad_ref[...], w_ref[...])
    total = each_row(lambda i, acc: acc + pre_ref[row_at(i), :], zeros())
    mean = col_sum(total) / SPOTS
    share(pair_rows(mean, spread_of(pre_ref, mean, valid_mask())), stat_ref)


def slide(parts, sign):
    out = parts[2]
    for b in (0, 1, 3, 4):
        out = out + pltpu.roll(parts[b], (sign * (2 - b)) % WIDE, 0)
    return out


def row_taps(halo_ref, taps, i, flip):
    parts = [None] * KER
    for a in range(KER):
        source = halo_ref[row_at(i + a), :].reshape(WIDE // 8, 8, LANES)
        for b in range(KER):
            term = source * taps[((KER - 1 - a) if flip else a) * KER + b]
            parts[b] = term if parts[b] is None else parts[b] + term
    return slide([part.reshape(WIDE, LANES) for part in parts], -1 if flip else 1)


def clear_halo(ref):
    edge = jnp.zeros((2 * WIDE, LANES), F32)
    ref[0 : 2 * WIDE, :] = edge
    ref[HALO - 2 * WIDE : HALO, :] = edge


def tap_rows(table_ref):
    return [jnp.broadcast_to(table_ref[k : k + 1, :], (8, LANES)) for k in range(KER * KER)]


def forward_kernel(
    xpad_ref, w_ref, gathered_ref, table_ref, depth_ref, stat_ref, moment_ref, pre_ref, halo_ref
):
    @pl.when(pl.program_id(0) == 0)
    def _():
        clear_halo(halo_ref)

    mask = valid_mask()
    center, scale = merged(gathered_ref[...])
    moment_ref[0:1, :] = center
    moment_ref[1:2, :] = scale
    slope = scale * table_ref[GAIN_ONE : GAIN_ONE + 1, :]
    offset = table_ref[SHIFT_ONE : SHIFT_ONE + 1, :] - center * slope
    pre_ref[...] = dot(xpad_ref[...], w_ref[...])

    def activate(i, _):
        act = pre_ref[row_at(i), :] * slope + offset
        silu = (act * logistic(act)).astype(BF16).astype(F32)
        halo_ref[row_at(i + 2), :] = jnp.where(mask, silu, 0.0)
        return 0

    each_row(activate, 0)
    taps = tap_rows(table_ref)

    def filter_row(i, acc):
        out = jnp.where(mask, row_taps(halo_ref, taps, i, False), 0.0)
        depth_ref[row_at(i), :] = out
        return acc + out

    mean = col_sum(each_row(filter_row, zeros())) / SPOTS
    share(pair_rows(mean, spread_of(depth_ref, mean, mask)), stat_ref)


def lanes_at(index):
    return pl.ds(pl.multiple_of(index * LANES, LANES), LANES)


def project_kernel(
    depth_ref,
    gathered_ref,
    table_ref,
    wproject_ref,
    cot_ref,
    wreduce_ref,
    wrestore_ref,
    breduce_ref,
    brestore_ref,
    moment_ref,
    project_ref,
    cpad_ref,
    vector_ref,
    column_ref,
    stat_ref,
    act_ref,
    hidden_ref,
    line_ref,
):
    step = pl.program_id(0)
    mask = valid_mask()
    center, scale = merged(gathered_ref[...])
    moment_ref[0:1, :] = center
    moment_ref[1:2, :] = scale
    slope = scale * table_ref[GAIN_TWO : GAIN_TWO + 1, :]
    offset = table_ref[SHIFT_TWO : SHIFT_TWO + 1, :] - center * slope

    def activate(i, acc):
        act = depth_ref[row_at(i), :] * slope + offset
        silu = jnp.where(mask, act * logistic(act), 0.0).astype(BF16)
        act_ref[step, row_at(i), :] = silu
        return acc + silu.astype(F32)

    vector_ref[0:1, lanes_at(step)] = col_sum(each_row(activate, zeros())) / SPOTS

    @pl.when(step == 0)
    def _():
        widen(cot_ref, cpad_ref, line_ref)

    @pl.when(step == CHUNKS - 1)
    def _():
        pooled = vector_ref[0:1, :]
        logit = jnp.sum(wreduce_ref[...] * pooled, axis=1, keepdims=True) + breduce_ref[...]
        squeezed = logit * logistic(logit)
        column_ref[0] = logit
        column_ref[1] = squeezed
        restored = col_sum(wrestore_ref[...] * squeezed[:, 0:1]) + brestore_ref[...]
        vector_ref[1:2, :] = logistic(restored)

        def project(c, _):
            excite = vector_ref[1:2, lanes_at(c)]

            def scale_row(i, _):
                hidden_ref[row_at(i), :] = (
                    act_ref[c, row_at(i), :].astype(F32) * excite
                ).astype(BF16)
                return 0

            each_row(scale_row, 0)
            part = dot(hidden_ref[...], wproject_ref[:, lanes_at(c)], 1, 1)

            @pl.when(c == 0)
            def _():
                project_ref[...] = part

            @pl.when(c > 0)
            def _():
                project_ref[...] += part

            return 0

        lax.fori_loop(0, CHUNKS, project, 0)

        def sums(i, accs):
            values, incoming = project_ref[row_at(i), :], cpad_ref[row_at(i), :].astype(F32)
            return accs[0] + values, accs[1] + incoming

        total, cot_total = each_row(sums, (zeros(C), zeros(C)))
        mean = col_sum(total) / SPOTS

        def devs(i, accs):
            dev = jnp.where(valid_mask(C), project_ref[row_at(i), :] - mean, 0.0)
            incoming = cpad_ref[row_at(i), :].astype(F32)
            return accs[0] + dev * dev, accs[1] + incoming * dev

        square, cross = each_row(devs, (zeros(C), zeros(C)))
        row = lax.broadcasted_iota(jnp.int32, (4, C), 0)
        packed = jnp.where(
            row == 0,
            mean,
            jnp.where(
                row == 1,
                col_sum(square) / SPOTS,
                jnp.where(row == 2, col_sum(cot_total), col_sum(cross)),
            ),
        )
        share(packed, stat_ref)


def back_project_kernel(
    depth_ref,
    gathered_ref,
    table_ref,
    moment_ref,
    project_ref,
    cpad_ref,
    gain_ref,
    wproject_ref,
    vector_ref,
    column_ref,
    wreduce_ref,
    wrestore_ref,
    first_ref,
    slope_ref,
    grads_ref,
    pooled_ref,
    stat_ref,
    gpp_ref,
    hidden_ref,
    back_ref,
    sums_ref,
    gain_sum_ref,
):
    step = pl.program_id(0)
    mask = valid_mask()

    @pl.when(step == 0)
    def _():
        gathered = gathered_ref[...]
        peers = gathered.shape[0]
        count = peers * SPOTS
        total = jnp.sum(gathered, axis=0)
        center3 = total[0:1] / peers
        away = gathered[:, 0:1, :] - center3[None]
        spread = (total[1:2] + jnp.sum(jnp.square(away), axis=0)) / peers
        scale3 = lax.rsqrt(spread + EPSILON)
        cross = total[3:4] + jnp.sum(gathered[:, 2:3, :] * away, axis=0)
        first = total[2:3] / count
        second = cross * scale3 / count
        factor = scale3 * gain_ref[...]
        wide = valid_mask(C)

        def body(i, acc):
            normed = (project_ref[row_at(i), :] - center3) * scale3
            incoming = cpad_ref[row_at(i), :].astype(F32)
            grad = factor * (incoming - first - normed * second)
            gpp_ref[row_at(i), :] = jnp.where(wide, grad, 0.0).astype(BF16)
            return acc + incoming * normed

        gain_sum_ref[...] = jnp.zeros_like(gain_sum_ref)
        gain_sum_ref[0:1, 0:C] = col_sum(each_row(body, zeros(C)))
        grads_ref[CHUNKS * EARLY :, :] = jnp.zeros((EARLY_ROWS - CHUNKS * EARLY, LANES), F32)

    center, scale = moment_ref[0:1, :], moment_ref[1:2, :]
    gain = table_ref[GAIN_TWO : GAIN_TWO + 1, :]
    shift = table_ref[SHIFT_TWO : SHIFT_TWO + 1, :]
    excite = vector_ref[1:2, lanes_at(step)]
    back_ref[...] = dot(gpp_ref[...], wproject_ref[...])

    def body(i, accs):
        normed = (depth_ref[row_at(i), :] - center) * scale
        act = normed * gain + shift
        sig = logistic(act)
        silu = (act * sig).astype(BF16).astype(F32)
        slope = jnp.where(mask, sig * (1.0 + act * (1.0 - sig)), 0.0)
        hidden_ref[row_at(i), :] = jnp.where(mask, silu * excite, 0.0).astype(BF16)
        back = back_ref[row_at(i), :]
        first = back * slope
        first_ref[row_at(i), :] = first
        slope_ref[row_at(i), :] = slope
        return (
            accs[0] + back * silu,
            accs[1] + first,
            accs[2] + first * normed,
            accs[3] + slope,
            accs[4] + slope * normed,
        )

    totals = each_row(body, tuple(zeros() for _ in range(5)))
    for k in range(5):
        sums_ref[k : k + 1, lanes_at(step)] = col_sum(totals[k])
    base = pl.multiple_of(step * EARLY, 16)
    grads_ref[pl.ds(base, C), :] = dot(gpp_ref[...], hidden_ref[...], 0, 0)

    @pl.when(step == CHUNKS - 1)
    def _():
        pooled, excite = vector_ref[0:1, :], vector_ref[1:2, :]
        logit, squeezed = column_ref[0], column_ref[1]
        grad_logit = sums_ref[0:1, :] * excite * (1.0 - excite)
        grad_squeezed = jnp.sum(wrestore_ref[...] * grad_logit, axis=1, keepdims=True)
        sig = logistic(logit)
        grad_reduce = grad_squeezed * (sig * (1.0 + logit * (1.0 - sig)))
        grad_pooled = col_sum(wreduce_ref[...] * grad_reduce[:, 0:1]) / SPOTS
        pooled_ref[0:1, :] = grad_pooled
        shift_sum = excite * sums_ref[1:2, :] + grad_pooled * sums_ref[3:4, :]
        gain_sum = excite * sums_ref[2:3, :] + grad_pooled * sums_ref[4:5, :]
        share(pair_rows(shift_sum, gain_sum), stat_ref)
        lane = lax.broadcasted_iota(jnp.int32, (SE_ROWS, LANES), 1)
        row = lax.broadcasted_iota(jnp.int32, (SE_ROWS, LANES), 0)
        bias_row = col_sum(jnp.where(lane == row, grad_reduce, 0.0))
        for c in range(CHUNKS):
            cut = slice(c * LANES, (c + 1) * LANES)
            block = squeezed * grad_logit[:, cut]
            block = jnp.where(row == SE, grad_logit[:, cut], block)
            block = jnp.where(row == SE + 1, shift_sum[:, cut], block)
            block = jnp.where(row == SE + 2, gain_sum[:, cut], block)
            extra = gain_sum_ref[0:1, cut] if c < 2 else bias_row
            block = jnp.where(row == SE + 3, extra, block)
            grads_ref[c * EARLY + C : c * EARLY + C + SE_ROWS, :] = block
            grads_ref[c * EARLY + C + SE_ROWS : (c + 1) * EARLY, :] = grad_reduce * pooled[:, cut]


def back_depth_kernel(
    depth_ref,
    first_ref,
    slope_ref,
    gathered_ref,
    table_ref,
    moment_two_ref,
    moment_one_ref,
    vector_ref,
    pooled_ref,
    xpad_ref,
    w_ref,
    grad_ref,
    stat_ref,
    sums_ref,
    pre_ref,
    halo_ref,
    ghalo_ref,
    side_ref,
):
    @pl.when(pl.program_id(0) == 0)
    def _():
        clear_halo(halo_ref)
        clear_halo(ghalo_ref)

    mask = valid_mask()
    total = jnp.sum(gathered_ref[...], axis=0)
    gain = table_ref[GAIN_TWO : GAIN_TWO + 1, :]
    count = gathered_ref.shape[0] * SPOTS
    mean_first = gain * total[0:1] / count
    mean_second = gain * total[1:2] / count
    center, scale = moment_two_ref[0:1, :], moment_two_ref[1:2, :]
    excite = vector_ref[1:2, :] * gain
    pooled = pooled_ref[0:1, :] * gain
    center_one, scale_one = moment_one_ref[0:1, :], moment_one_ref[1:2, :]
    slope_one = scale_one * table_ref[GAIN_ONE : GAIN_ONE + 1, :]
    offset_one = table_ref[SHIFT_ONE : SHIFT_ONE + 1, :] - center_one * slope_one
    pre_ref[...] = dot(xpad_ref[...], w_ref[...])

    def prepare(i, _):
        normed = (depth_ref[row_at(i), :] - center) * scale
        grad = first_ref[row_at(i), :] * excite + slope_ref[row_at(i), :] * pooled
        grad = scale * (grad - mean_first - normed * mean_second)
        ghalo_ref[row_at(i + 2), :] = jnp.where(mask, grad, 0.0)
        act = pre_ref[row_at(i), :] * slope_one + offset_one
        sig = logistic(act)
        silu = (act * sig).astype(BF16).astype(F32)
        halo_ref[row_at(i + 2), :] = jnp.where(mask, silu, 0.0)
        side_ref[row_at(i), :] = jnp.where(mask, sig * (1.0 + act * (1.0 - sig)), 0.0)
        return 0

    each_row(prepare, 0)

    def kernel_grad(i, accs):
        grad = ghalo_ref[row_at(i + 2), :]
        shifted = [
            (grad if b == 2 else pltpu.roll(grad, (b - 2) % WIDE, 0)).reshape(
                WIDE // 8, 8, LANES
            )
            for b in range(KER)
        ]
        accs = list(accs)
        for a in range(KER):
            field = halo_ref[row_at(i + a), :].reshape(WIDE // 8, 8, LANES)
            for b in range(KER):
                accs[a * KER + b] = accs[a * KER + b] + jnp.sum(field * shifted[b], axis=0)
        return tuple(accs)

    start = tuple(jnp.zeros((8, LANES), F32) for _ in range(KER * KER))
    accs = each_row(kernel_grad, start)
    for k in range(KER * KER):
        sums_ref[k : k + 1, :] = col_sum(accs[k])
    taps = tap_rows(table_ref)

    def input_grad(i, accs):
        grad = row_taps(ghalo_ref, taps, i, True) * side_ref[row_at(i), :]
        grad_ref[row_at(i), :] = grad
        normed = (pre_ref[row_at(i), :] - center_one) * scale_one
        return accs[0] + grad, accs[1] + grad * normed

    shift_sum, gain_sum = (col_sum(a) for a in each_row(input_grad, (zeros(), zeros())))
    share(pair_rows(shift_sum, gain_sum), stat_ref)
    sums_ref[KER * KER : TABLE, :] = jnp.zeros((TABLE - KER * KER, LANES), F32)
    sums_ref[25:26, :] = shift_sum
    sums_ref[26:27, :] = gain_sum


def back_expand_kernel(
    grad_ref,
    gathered_ref,
    table_ref,
    moment_ref,
    xpad_ref,
    w_ref,
    sums_ref,
    cpad_ref,
    out_ref,
    grads_ref,
    pre_ref,
    gpe_ref,
    acc_ref,
):
    step = pl.program_id(0)
    mask = valid_mask()
    total = jnp.sum(gathered_ref[...], axis=0)
    count = gathered_ref.shape[0] * SPOTS
    mean_first, mean_second = total[0:1] / count, total[1:2] / count
    center, scale = moment_ref[0:1, :], moment_ref[1:2, :]
    factor = scale * table_ref[GAIN_ONE : GAIN_ONE + 1, :]
    pre_ref[...] = dot(xpad_ref[...], w_ref[...])

    def body(i, _):
        normed = (pre_ref[row_at(i), :] - center) * scale
        grad = factor * (grad_ref[row_at(i), :] - mean_first - normed * mean_second)
        gpe_ref[row_at(i), :] = jnp.where(mask, grad, 0.0).astype(BF16)
        return 0

    each_row(body, 0)
    base = pl.multiple_of(step * LATE, 16)
    grads_ref[pl.ds(base, C), :] = dot(xpad_ref[...], gpe_ref[...], 0, 0)
    grads_ref[pl.ds(pl.multiple_of(base + C, 16), TABLE), :] = sums_ref[...]
    part = dot(gpe_ref[...], w_ref[...], 1, 1)

    @pl.when(step == 0)
    def _():
        acc_ref[...] = cpad_ref[...].astype(F32) + part
        grads_ref[CHUNKS * LATE :, :] = jnp.zeros((LATE_ROWS - CHUNKS * LATE, LANES), F32)

    @pl.when(step > 0)
    def _():
        acc_ref[...] += part

    @pl.when(step == CHUNKS - 1)
    def _():
        for i in range(SIDE):
            out_ref[i] = acc_ref[i * WIDE : i * WIDE + SIDE, :].astype(BF16)


def put_row(ref, rows_ref, row, height, scale):
    for c in range(-(-ref.shape[1] // LANES)):
        width = min(LANES, ref.shape[1] - c * LANES)
        at = c * height + row
        ref[:, c * LANES : c * LANES + width] = rows_ref[at : at + ref.shape[0], 0:width] * scale


def unpack_early_kernel(
    scale, rows_ref, project_ref, restore_ref, reduce_ref, brestore_ref, shift_ref, gain_ref,
    gproject_ref, breduce_ref,
):
    put_row(project_ref, rows_ref, 0, EARLY, scale)
    put_row(restore_ref, rows_ref, C, EARLY, scale)
    put_row(reduce_ref, rows_ref, C + SE_ROWS, EARLY, scale)
    put_row(brestore_ref, rows_ref, C + SE, EARLY, scale)
    put_row(shift_ref, rows_ref, C + SE + 1, EARLY, scale)
    put_row(gain_ref, rows_ref, C + SE + 2, EARLY, scale)
    put_row(gproject_ref, rows_ref, C + SE + 3, EARLY, scale)
    at = 2 * EARLY + C + SE + 3
    breduce_ref[...] = rows_ref[at : at + 1, 0:SE] * scale


def unpack_late_kernel(scale, rows_ref, expand_ref, depth_ref, shift_ref, gain_ref):
    put_row(expand_ref, rows_ref, 0, LATE, scale)
    put_row(depth_ref, rows_ref, C, LATE, scale)
    put_row(shift_ref, rows_ref, C + 25, LATE, scale)
    put_row(gain_ref, rows_ref, C + 26, LATE, scale)


def unpack(kernel, rows, shapes, scale):
    return pl.pallas_call(
        functools.partial(kernel, scale),
        out_shape=tuple(f32(*shape) for shape in shapes),
        compiler_params=pltpu.CompilerParams(vmem_limit_bytes=40 * 2**20),
        cost_estimate=pl.CostEstimate(
            flops=rows.size, bytes_accessed=8 * rows.size, transcendentals=0
        ),
    )(rows)


def whole(shape):
    return pl.BlockSpec(shape, lambda c: (0,) * len(shape))


def lane_block(rows):
    return pl.BlockSpec((rows, LANES), lambda c: (0, c))


def peer_block(peers):
    return pl.BlockSpec((peers, 2, LANES), lambda c: (0, 0, c))


MAP_BLOCK = pl.BlockSpec((pl.squeezed, ROWS, LANES), lambda c: (c, 0, 0))
MAP = jax.ShapeDtypeStruct((CHUNKS, ROWS, LANES), F32)
EDGE = jax.ShapeDtypeStruct((ROWS, C), F32)
EDGE_BF16 = jax.ShapeDtypeStruct((ROWS, C), BF16)


def f32(*shape):
    return jax.ShapeDtypeStruct(shape, F32)


def call(kernel, ins, outs, scratch, flops):
    return pl.pallas_call(
        kernel,
        grid=(CHUNKS,),
        in_specs=ins,
        out_specs=tuple(spec for spec, _ in outs),
        out_shape=tuple(shape for _, shape in outs),
        scratch_shapes=scratch,
        compiler_params=pltpu.CompilerParams(vmem_limit_bytes=40 * 2**20),
        cost_estimate=pl.CostEstimate(
            flops=flops, bytes_accessed=12 * 2**20, transcendentals=ROWS * PADDED
        ),
    )


def exchange(copies, axes):
    return lax.all_to_all(copies, axes, 0, 0, tiled=True)


def plane_parts(rows):
    plane = lax.axis_size(PLANE)
    parts = exchange(rows.reshape(plane, rows.shape[0] // plane, LANES), PLANE)
    return jnp.sum(parts, axis=0)


def depth_parts(mine):
    depth = lax.axis_size("z")
    return jnp.sum(exchange(jnp.broadcast_to(mine[None], (depth,) + mine.shape), "z"), axis=0)


def plane_whole(mine):
    plane = lax.axis_size(PLANE)
    return exchange(jnp.broadcast_to(mine[None], (plane,) + mine.shape), PLANE).reshape(-1, LANES)


def tie(first, second):
    return lax.optimization_barrier((first, second))


def per_device(
    block_input,
    cotangent,
    w_expand,
    gain_expand,
    shift_expand,
    w_depth,
    gain_depth,
    shift_depth,
    w_reduce,
    b_reduce,
    w_restore,
    b_restore,
    w_project,
    gain_project,
    upper_grads,
):
    peers = lax.axis_size(GROUP)
    images_total = lax.axis_size(AXES)
    extra = PADDED - HID
    images, cot = block_input[0, 0], cotangent[0, 0]
    wexp = jnp.pad(w_expand, ((0, 0), (0, extra)))
    wproj = jnp.pad(w_project.T, ((0, 0), (0, extra)))
    wred = jnp.pad(w_reduce.astype(F32).T, ((0, SE_ROWS - SE), (0, extra)))
    wres = jnp.pad(w_restore.astype(F32), ((0, SE_ROWS - SE), (0, extra)))
    bred = jnp.broadcast_to(jnp.pad(b_reduce, (0, SE_ROWS - SE))[:, None], (SE_ROWS, LANES))
    bres = jnp.pad(b_restore, (0, extra))[None]
    table = jnp.concatenate(
        [w_depth.astype(F32)]
        + [v[None] for v in (gain_expand, shift_expand, gain_depth, shift_depth)],
        axis=0,
    )
    table = jnp.pad(table, ((0, TABLE - table.shape[0]), (0, extra)))
    xpad_spec, w_spec = whole((ROWS, C)), lane_block(C)
    se_spec = whole((SE_ROWS, PADDED))
    stat_out = (peer_block(peers), f32(peers, 2, PADDED))
    stat_whole = (whole((peers, 2, PADDED)), f32(peers, 2, PADDED))
    moments = (lane_block(8), f32(8, PADDED))
    map_f32 = pltpu.VMEM((ROWS, LANES), F32)
    map_bf16 = pltpu.VMEM((ROWS, LANES), BF16)
    line = pltpu.VMEM((2, WIDE, C), F32)
    halo = pltpu.VMEM((HALO, LANES), F32)
    matmul = 2 * ROWS * C * PADDED

    xpad, stat = call(
        stats_kernel,
        [whole((SIDE, SIDE, C)), w_spec],
        [(xpad_spec, EDGE_BF16), stat_out],
        [map_f32, line],
        matmul,
    )(images, wexp)
    gathered = exchange(stat, GROUP)
    upper = plane_parts(upper_grads[0].reshape(-1, LANES))
    depth, stat, moment_one = call(
        forward_kernel,
        [xpad_spec, w_spec, peer_block(peers), lane_block(TABLE)],
        [(MAP_BLOCK, MAP), stat_out, moments],
        [map_f32, halo],
        50 * ROWS * PADDED,
    )(xpad, wexp, gathered, table)
    stat, upper = tie(stat, upper)
    gathered = exchange(stat, GROUP)
    upper = depth_parts(upper)
    moment_two, project, cpad, vector, column, stat = call(
        project_kernel,
        [
            MAP_BLOCK,
            peer_block(peers),
            lane_block(TABLE),
            whole((C, PADDED)),
            whole((SIDE, SIDE, C)),
            se_spec,
            se_spec,
            whole((SE_ROWS, LANES)),
            whole((1, PADDED)),
        ],
        [
            moments,
            (whole((ROWS, C)), EDGE),
            (whole((ROWS, C)), EDGE_BF16),
            (whole((8, PADDED)), f32(8, PADDED)),
            (whole((2, SE_ROWS, LANES)), f32(2, SE_ROWS, LANES)),
            (whole((peers, 4, C)), f32(peers, 4, C)),
        ],
        [pltpu.VMEM((CHUNKS, ROWS, LANES), BF16), map_bf16, line],
        matmul,
    )(depth, gathered, table, wproj, cot, wred, wres, bred, bres)
    stat, upper = tie(stat, upper)
    gathered = exchange(stat, GROUP)
    upper = plane_whole(upper)
    first, slope, early, pooled, stat = call(
        back_project_kernel,
        [
            MAP_BLOCK,
            whole((peers, 4, C)),
            lane_block(TABLE),
            lane_block(8),
            whole((ROWS, C)),
            whole((ROWS, C)),
            whole((1, C)),
            w_spec,
            whole((8, PADDED)),
            whole((2, SE_ROWS, LANES)),
            se_spec,
            se_spec,
        ],
        [
            (MAP_BLOCK, MAP),
            (MAP_BLOCK, MAP),
            (whole((EARLY_ROWS, LANES)), f32(EARLY_ROWS, LANES)),
            (whole((8, PADDED)), f32(8, PADDED)),
            stat_whole,
        ],
        [
            pltpu.VMEM((ROWS, C), BF16),
            map_bf16,
            map_f32,
            pltpu.VMEM((8, PADDED), F32),
            pltpu.VMEM((8, 2 * LANES), F32),
        ],
        2 * matmul,
    )(
        depth,
        gathered,
        table,
        moment_two,
        project,
        cpad,
        gain_project[None],
        wproj,
        vector,
        column,
        wred,
        wres,
    )
    stat, upper = tie(stat, upper)
    gathered = exchange(stat, GROUP)
    early = plane_parts(early)
    grad_one, stat, sums = call(
        back_depth_kernel,
        [
            MAP_BLOCK,
            MAP_BLOCK,
            MAP_BLOCK,
            peer_block(peers),
            lane_block(TABLE),
            lane_block(8),
            lane_block(8),
            lane_block(8),
            lane_block(8),
            xpad_spec,
            w_spec,
        ],
        [(MAP_BLOCK, MAP), stat_out, (lane_block(TABLE), f32(TABLE, PADDED))],
        [map_f32, halo, halo, map_f32],
        100 * ROWS * PADDED,
    )(depth, first, slope, gathered, table, moment_two, moment_one, vector, pooled, xpad, wexp)
    stat, early = tie(stat, early)
    gathered = exchange(stat, GROUP)
    early = depth_parts(early)
    input_grad, late = call(
        back_expand_kernel,
        [
            MAP_BLOCK,
            peer_block(peers),
            lane_block(TABLE),
            lane_block(8),
            xpad_spec,
            w_spec,
            lane_block(TABLE),
            xpad_spec,
        ],
        [
            (whole((SIDE, SIDE, C)), jax.ShapeDtypeStruct((SIDE, SIDE, C), BF16)),
            (whole((LATE_ROWS, LANES)), f32(LATE_ROWS, LANES)),
        ],
        [map_f32, map_bf16, pltpu.VMEM((ROWS, C), F32)],
        3 * matmul,
    )(grad_one, gathered, table, moment_one, xpad, wexp, sums, cpad)

    late, early = tie(late, early)
    late = plane_parts(late)
    early = plane_whole(early)
    late, early = tie(late, early)
    late = plane_whole(depth_parts(late))

    scale = 1.0 / images_total
    wide = (1, HID)
    g_project, g_restore, g_reduce, g_brestore, g_shift_two, g_gain_two, g_gproject, g_breduce = (
        unpack(
            unpack_early_kernel,
            early,
            [(C, HID), (SE, HID), (SE, HID), wide, wide, wide, (1, C), (1, SE)],
            scale,
        )
    )
    g_expand, g_depth, g_shift_one, g_gain_one = unpack(
        unpack_late_kernel, late, [(C, HID), (KER * KER, HID), wide, wide], scale
    )
    return (
        input_grad[None, None],
        g_expand,
        g_gain_one[0],
        g_shift_one[0],
        g_depth,
        g_gain_two[0],
        g_shift_two[0],
        g_reduce.T,
        g_breduce[0],
        g_restore,
        g_brestore[0],
        g_project.T,
        g_gproject[0],
        upper.reshape(-1),
    )


def solution(mesh):
    chips = Mesh(mesh.devices.reshape(SHAPE), AXES)
    maps = P(("z", "core"), GROUP, None, None, None)
    return jax.shard_map(
        per_device,
        mesh=chips,
        in_specs=(maps, maps) + (P(),) * 12 + (P(AXES, None),),
        out_specs=(maps,) + (P(),) * 13,
        check_vma=False,
    )
```

```python
import functools

import jax
import jax.numpy as jnp
from jax import lax
from jax.experimental import pallas as pl
from jax.experimental.pallas import tpu as pltpu
from jax.sharding import Mesh, PartitionSpec as P

KER = 5
EPSILON = 0.001
SHAPE = (4, 8, 8, 2)
AXES = ("x", "y", "z", "core")
GROUP = ("x", "y")
CHIPS = ("x", "y", "z")
SIDE = 29
WIDE = 32
ROWS = SIDE * WIDE
HALO = (SIDE + KER - 1) * WIDE
C = 176
HID = 1056
LANES = 128
CHUNKS = 9
PADDED = CHUNKS * LANES
SE = 44
SE_ROWS = 48
SPOTS = SIDE * SIDE
GAIN_ONE, SHIFT_ONE, GAIN_TWO, SHIFT_TWO, BIAS = 25, 26, 27, 28, 29
TABLE = 32
EARLY = C + 2 * SE_ROWS
UPPER_AT = CHUNKS * EARLY
UPPER_ROWS = 1024
EARLY_ROWS = 4096
LATE = C + TABLE
LATE_ROWS = 2048
PIECE = 4
F32 = jnp.float32
BF16 = jnp.bfloat16


def dot(left, right, left_dim=1, right_dim=0):
    return lax.dot_general(
        left, right, (((left_dim,), (right_dim,)), ((), ())), preferred_element_type=F32
    )


def logistic(values):
    return 0.5 + 0.5 * jnp.tanh(0.5 * values)


def valid_mask(lanes=LANES):
    return lax.broadcasted_iota(jnp.int32, (WIDE, lanes), 0) < SIDE


def row_at(index):
    if isinstance(index, int):
        return slice(index * WIDE, (index + 1) * WIDE)
    return pl.ds(pl.multiple_of(index * WIDE, WIDE), WIDE)


def each_row(body, init):
    for i in range(SIDE):
        init = body(i, init)
    return init


def loop_rows(body, init):
    return lax.fori_loop(0, SIDE, body, init)


def col_sum(values):
    return jnp.sum(values, axis=0, keepdims=True)


def zeros(lanes=LANES):
    return jnp.zeros((WIDE, lanes), F32)


def share(pair, ref):
    ref[...] = jnp.broadcast_to(pair[None], ref.shape)


def pair_rows(first, second):
    return jnp.where(lax.broadcasted_iota(jnp.int32, (2, first.shape[1]), 0) == 0, first, second)


def spread_of(ref, mean, mask):
    def body(i, acc):
        dev = jnp.where(mask, ref[row_at(i), :] - mean, 0.0)
        return acc + dev * dev

    return col_sum(each_row(body, zeros(mean.shape[1]))) / SPOTS


def merged(gathered):
    peers = gathered.shape[0]
    total = jnp.sum(gathered, axis=0)
    center = total[0:1] / peers
    dev = jnp.sum(jnp.square(gathered[:, 0:1, :] - center[None]), axis=0)
    spread = (total[1:2] + dev) / peers
    return center, lax.rsqrt(spread + EPSILON)


def widen(map_ref, flat_ref, line_ref):
    line_ref[...] = jnp.zeros_like(line_ref)
    for i in range(SIDE):
        line_ref[i % 2, 0:SIDE, :] = map_ref[i].astype(F32)
        flat_ref[i * WIDE : (i + 1) * WIDE, :] = line_ref[i % 2].astype(BF16)


def stats_kernel(x_ref, w_ref, xpad_ref, stat_ref, pre_ref, line_ref):
    @pl.when(pl.program_id(0) == 0)
    def _():
        widen(x_ref, xpad_ref, line_ref)

    pre_ref[...] = dot(xpad_ref[...], w_ref[...])
    total = each_row(lambda i, acc: acc + pre_ref[row_at(i), :], zeros())
    mean = col_sum(total) / SPOTS
    share(pair_rows(mean, spread_of(pre_ref, mean, valid_mask())), stat_ref)


def slide(parts, sign):
    out = parts[2]
    for b in (0, 1, 3, 4):
        out = out + pltpu.roll(parts[b], (sign * (2 - b)) % WIDE, 0)
    return out


def row_taps(halo_ref, tap_ref, i, flip):
    parts = [None] * KER
    for a in range(KER):
        source = halo_ref[row_at(i + a), :].reshape(WIDE // 8, 8, LANES)
        for b in range(KER):
            k = ((KER - 1 - a) if flip else a) * KER + b
            term = source * tap_ref[k * 8 : k * 8 + 8, :]
            parts[b] = term if parts[b] is None else parts[b] + term
    return slide([part.reshape(WIDE, LANES) for part in parts], -1 if flip else 1)


def clear_halo(ref):
    edge = jnp.zeros((2 * WIDE, LANES), F32)
    ref[0 : 2 * WIDE, :] = edge
    ref[HALO - 2 * WIDE : HALO, :] = edge


def spread_taps(table_ref, tap_ref):
    for k in range(KER * KER):
        tap_ref[k * 8 : k * 8 + 8, :] = jnp.broadcast_to(table_ref[k : k + 1, :], (8, LANES))


def forward_kernel(
    xpad_ref,
    w_ref,
    gathered_ref,
    table_ref,
    depth_ref,
    stat_ref,
    moment_ref,
    pre_ref,
    halo_ref,
    tap_ref,
):
    @pl.when(pl.program_id(0) == 0)
    def _():
        clear_halo(halo_ref)

    mask = valid_mask()
    center, scale = merged(gathered_ref[...])
    moment_ref[0:1, :] = center
    moment_ref[1:2, :] = scale
    slope = scale * table_ref[GAIN_ONE : GAIN_ONE + 1, :]
    offset = table_ref[SHIFT_ONE : SHIFT_ONE + 1, :] - center * slope
    pre_ref[...] = dot(xpad_ref[...], w_ref[...])

    def activate(i, _):
        act = pre_ref[row_at(i), :] * slope + offset
        silu = (act * logistic(act)).astype(BF16).astype(F32)
        halo_ref[row_at(i + 2), :] = jnp.where(mask, silu, 0.0)
        return 0

    each_row(activate, 0)
    spread_taps(table_ref, tap_ref)

    def filter_row(i, acc):
        out = jnp.where(mask, row_taps(halo_ref, tap_ref, i, False), 0.0)
        depth_ref[row_at(i), :] = out
        return acc + out

    mean = col_sum(loop_rows(filter_row, zeros())) / SPOTS
    share(pair_rows(mean, spread_of(depth_ref, mean, mask)), stat_ref)


def lanes_at(index):
    return pl.ds(pl.multiple_of(index * LANES, LANES), LANES)


def project_kernel(
    depth_ref,
    gathered_ref,
    table_ref,
    wproject_ref,
    cot_ref,
    wreduce_ref,
    wrestore_ref,
    breduce_ref,
    brestore_ref,
    moment_ref,
    project_ref,
    cpad_ref,
    vector_ref,
    column_ref,
    stat_ref,
    act_ref,
    hidden_ref,
    line_ref,
):
    step = pl.program_id(0)
    mask = valid_mask()
    center, scale = merged(gathered_ref[...])
    moment_ref[0:1, :] = center
    moment_ref[1:2, :] = scale
    slope = scale * table_ref[GAIN_TWO : GAIN_TWO + 1, :]
    offset = table_ref[SHIFT_TWO : SHIFT_TWO + 1, :] - center * slope

    def activate(i, acc):
        act = depth_ref[row_at(i), :] * slope + offset
        silu = jnp.where(mask, act * logistic(act), 0.0).astype(BF16)
        act_ref[step, row_at(i), :] = silu
        return acc + silu.astype(F32)

    vector_ref[0:1, lanes_at(step)] = col_sum(each_row(activate, zeros())) / SPOTS

    @pl.when(step == 0)
    def _():
        widen(cot_ref, cpad_ref, line_ref)

    @pl.when(step == CHUNKS - 1)
    def _():
        pooled = vector_ref[0:1, :]
        logit = jnp.sum(wreduce_ref[...] * pooled, axis=1, keepdims=True) + breduce_ref[...]
        squeezed = logit * logistic(logit)
        column_ref[0] = logit
        column_ref[1] = squeezed
        restored = col_sum(wrestore_ref[...] * squeezed[:, 0:1]) + brestore_ref[...]
        vector_ref[1:2, :] = logistic(restored)

        def fill(c, _):
            excite = vector_ref[1:2, lanes_at(c)]

            def scale_row(i, _):
                hidden_ref[row_at(i), lanes_at(c)] = (
                    act_ref[c, row_at(i), :].astype(F32) * excite
                ).astype(BF16)
                return 0

            each_row(scale_row, 0)
            return 0

        lax.fori_loop(0, CHUNKS, fill, 0)
        project_ref[...] = dot(hidden_ref[...], wproject_ref[...])

        def sums(i, accs):
            values, incoming = project_ref[row_at(i), :], cpad_ref[row_at(i), :].astype(F32)
            return accs[0] + values, accs[1] + incoming

        total, cot_total = each_row(sums, (zeros(C), zeros(C)))
        mean = col_sum(total) / SPOTS

        def devs(i, accs):
            dev = jnp.where(valid_mask(C), project_ref[row_at(i), :] - mean, 0.0)
            incoming = cpad_ref[row_at(i), :].astype(F32)
            return accs[0] + dev * dev, accs[1] + incoming * dev

        square, cross = each_row(devs, (zeros(C), zeros(C)))
        row = lax.broadcasted_iota(jnp.int32, (4, C), 0)
        packed = jnp.where(
            row == 0,
            mean,
            jnp.where(
                row == 1,
                col_sum(square) / SPOTS,
                jnp.where(row == 2, col_sum(cot_total), col_sum(cross)),
            ),
        )
        share(packed, stat_ref)


def back_project_kernel(
    depth_ref,
    gathered_ref,
    table_ref,
    moment_ref,
    project_ref,
    cpad_ref,
    gain_ref,
    wproject_ref,
    vector_ref,
    column_ref,
    wreduce_ref,
    wrestore_ref,
    first_ref,
    slope_ref,
    hidden_ref,
    gpp_ref,
    row_ref,
    reduce_ref,
    stat_ref,
    back_ref,
    sums_ref,
):
    step = pl.program_id(0)
    mask = valid_mask()

    @pl.when(step == 0)
    def _():
        gathered = gathered_ref[...]
        peers = gathered.shape[0]
        count = peers * SPOTS
        total = jnp.sum(gathered, axis=0)
        center3 = total[0:1] / peers
        away = gathered[:, 0:1, :] - center3[None]
        spread = (total[1:2] + jnp.sum(jnp.square(away), axis=0)) / peers
        scale3 = lax.rsqrt(spread + EPSILON)
        cross = total[3:4] + jnp.sum(gathered[:, 2:3, :] * away, axis=0)
        first = total[2:3] / count
        second = cross * scale3 / count
        factor = scale3 * gain_ref[...]
        wide = valid_mask(C)

        def body(i, acc):
            normed = (project_ref[row_at(i), :] - center3) * scale3
            incoming = cpad_ref[row_at(i), :].astype(F32)
            grad = factor * (incoming - first - normed * second)
            gpp_ref[row_at(i), :] = jnp.where(wide, grad, 0.0).astype(BF16)
            return acc + incoming * normed

        row_ref[...] = jnp.zeros_like(row_ref)
        row_ref[4:5, 0:C] = col_sum(each_row(body, zeros(C)))

    center, scale = moment_ref[0:1, :], moment_ref[1:2, :]
    gain = table_ref[GAIN_TWO : GAIN_TWO + 1, :]
    shift = table_ref[SHIFT_TWO : SHIFT_TWO + 1, :]
    excite = vector_ref[1:2, lanes_at(step)]
    back_ref[...] = dot(gpp_ref[...], wproject_ref[...])

    def body(i, accs):
        normed = (depth_ref[row_at(i), :] - center) * scale
        act = normed * gain + shift
        sig = logistic(act)
        silu = (act * sig).astype(BF16).astype(F32)
        slope = jnp.where(mask, sig * (1.0 + act * (1.0 - sig)), 0.0)
        hidden_ref[row_at(i), :] = jnp.where(mask, silu * excite, 0.0).astype(BF16)
        back = back_ref[row_at(i), :]
        first = back * slope
        first_ref[row_at(i), :] = first
        slope_ref[row_at(i), :] = slope
        return (
            accs[0] + back * silu,
            accs[1] + first,
            accs[2] + first * normed,
            accs[3] + slope,
            accs[4] + slope * normed,
        )

    totals = each_row(body, tuple(zeros() for _ in range(5)))
    for k in range(5):
        sums_ref[k : k + 1, lanes_at(step)] = col_sum(totals[k])

    @pl.when(step == CHUNKS - 1)
    def _():
        excite = vector_ref[1:2, :]
        logit = column_ref[0]
        grad_logit = sums_ref[0:1, :] * excite * (1.0 - excite)
        grad_squeezed = jnp.sum(wrestore_ref[...] * grad_logit, axis=1, keepdims=True)
        sig = logistic(logit)
        grad_reduce = grad_squeezed * (sig * (1.0 + logit * (1.0 - sig)))
        grad_pooled = col_sum(wreduce_ref[...] * grad_reduce[:, 0:1]) / SPOTS
        shift_sum = excite * sums_ref[1:2, :] + grad_pooled * sums_ref[3:4, :]
        gain_sum = excite * sums_ref[2:3, :] + grad_pooled * sums_ref[4:5, :]
        share(pair_rows(shift_sum, gain_sum), stat_ref)
        row_ref[0:1, :] = grad_pooled
        row_ref[1:2, :] = grad_logit
        row_ref[2:3, :] = shift_sum
        row_ref[3:4, :] = gain_sum
        reduce_ref[...] = grad_reduce


def early_kernel(
    gpp_ref, hidden_ref, row_ref, reduce_ref, vector_ref, column_ref, upper_ref, grads_ref
):
    step = pl.program_id(0)
    base = pl.multiple_of(step * EARLY, 16)
    grads_ref[pl.ds(base, C), :] = dot(gpp_ref[...], hidden_ref[...], 0, 0)
    lane = lax.broadcasted_iota(jnp.int32, (SE_ROWS, LANES), 1)
    row = lax.broadcasted_iota(jnp.int32, (SE_ROWS, LANES), 0)
    squeezed, grad_reduce = column_ref[1], reduce_ref[...]
    block = squeezed * row_ref[1:2, :]
    block = jnp.where(row == SE, row_ref[1:2, :], block)
    block = jnp.where(row == SE + 1, row_ref[2:3, :], block)
    block = jnp.where(row == SE + 2, row_ref[3:4, :], block)
    bias_row = col_sum(jnp.where(lane == row, grad_reduce, 0.0))
    extra = jnp.where(step < 2, row_ref[4:5, :], bias_row)
    block = jnp.where(row == SE + 3, extra, block)
    grads_ref[pl.ds(pl.multiple_of(base + C, 16), SE_ROWS), :] = block
    grads_ref[pl.ds(pl.multiple_of(base + C + SE_ROWS, 16), SE_ROWS), :] = (
        grad_reduce * vector_ref[0:1, :]
    )

    @pl.when(step == 0)
    def _():
        grads_ref[UPPER_AT : UPPER_AT + UPPER_ROWS, :] = upper_ref[...]
        rest = EARLY_ROWS - UPPER_AT - UPPER_ROWS
        grads_ref[UPPER_AT + UPPER_ROWS :, :] = jnp.zeros((rest, LANES), F32)


def back_depth_kernel(
    depth_ref,
    first_ref,
    slope_ref,
    gathered_ref,
    table_ref,
    moment_two_ref,
    moment_one_ref,
    vector_ref,
    pooled_ref,
    xpad_ref,
    w_ref,
    grad_ref,
    stat_ref,
    sums_ref,
    field_ref,
    back_ref,
    pre_ref,
    ghalo_ref,
    side_ref,
    tap_ref,
):
    @pl.when(pl.program_id(0) == 0)
    def _():
        clear_halo(ghalo_ref)

    mask = valid_mask()
    total = jnp.sum(gathered_ref[...], axis=0)
    gain = table_ref[GAIN_TWO : GAIN_TWO + 1, :]
    count = gathered_ref.shape[0] * SPOTS
    mean_first = gain * total[0:1] / count
    mean_second = gain * total[1:2] / count
    center, scale = moment_two_ref[0:1, :], moment_two_ref[1:2, :]
    excite = vector_ref[1:2, :] * gain
    pooled = pooled_ref[0:1, :] * gain
    center_one, scale_one = moment_one_ref[0:1, :], moment_one_ref[1:2, :]
    slope_one = scale_one * table_ref[GAIN_ONE : GAIN_ONE + 1, :]
    offset_one = table_ref[SHIFT_ONE : SHIFT_ONE + 1, :] - center_one * slope_one
    pre_ref[...] = dot(xpad_ref[...], w_ref[...])

    def prepare(i, _):
        normed = (depth_ref[row_at(i), :] - center) * scale
        grad = first_ref[row_at(i), :] * excite + slope_ref[row_at(i), :] * pooled
        grad = jnp.where(mask, scale * (grad - mean_first - normed * mean_second), 0.0)
        ghalo_ref[row_at(i + 2), :] = grad
        back_ref[row_at(i), :] = grad
        act = pre_ref[row_at(i), :] * slope_one + offset_one
        sig = logistic(act)
        field_ref[row_at(i), :] = jnp.where(mask, act * sig, 0.0).astype(BF16)
        side_ref[row_at(i), :] = jnp.where(mask, sig * (1.0 + act * (1.0 - sig)), 0.0)
        return 0

    each_row(prepare, 0)
    spread_taps(table_ref, tap_ref)

    def input_grad(i, accs):
        grad = row_taps(ghalo_ref, tap_ref, i, True) * side_ref[row_at(i), :]
        grad_ref[row_at(i), :] = grad
        normed = (pre_ref[row_at(i), :] - center_one) * scale_one
        return accs[0] + grad, accs[1] + grad * normed

    shift_sum, gain_sum = (col_sum(a) for a in loop_rows(input_grad, (zeros(), zeros())))
    share(pair_rows(shift_sum, gain_sum), stat_ref)
    sums_ref[...] = jnp.zeros_like(sums_ref)
    sums_ref[0:1, :] = shift_sum
    sums_ref[1:2, :] = gain_sum


def kernel_grad_kernel(field_ref, back_ref, sums_ref, out_ref, halo_ref):
    @pl.when(pl.program_id(0) == 0)
    def _():
        clear_halo(halo_ref)

    halo_ref[2 * WIDE : 2 * WIDE + ROWS, :] = field_ref[...].astype(F32)

    def kernel_grad(i, accs):
        grad = back_ref[row_at(i), :]
        shifted = [
            (grad if b == 2 else pltpu.roll(grad, (b - 2) % WIDE, 0)).reshape(
                WIDE // 8, 8, LANES
            )
            for b in range(KER)
        ]
        accs = list(accs)
        for a in range(KER):
            field = halo_ref[row_at(i + a), :].reshape(WIDE // 8, 8, LANES)
            for b in range(KER):
                accs[a * KER + b] = accs[a * KER + b] + jnp.sum(field * shifted[b], axis=0)
        return tuple(accs)

    start = tuple(jnp.zeros((8, LANES), F32) for _ in range(KER * KER))
    accs = loop_rows(kernel_grad, start)
    for k in range(KER * KER):
        out_ref[k : k + 1, :] = col_sum(accs[k])
    out_ref[25:TABLE, :] = sums_ref[0 : TABLE - 25, :]


def back_expand_kernel(
    grad_ref,
    gathered_ref,
    table_ref,
    moment_ref,
    xpad_ref,
    w_ref,
    sums_ref,
    cpad_ref,
    xturn_ref,
    wturn_ref,
    out_ref,
    grads_ref,
    pre_ref,
    gpe_ref,
    acc_ref,
):
    step = pl.program_id(0)
    mask = valid_mask()
    total = jnp.sum(gathered_ref[...], axis=0)
    count = gathered_ref.shape[0] * SPOTS
    mean_first, mean_second = total[0:1] / count, total[1:2] / count
    center, scale = moment_ref[0:1, :], moment_ref[1:2, :]
    factor = scale * table_ref[GAIN_ONE : GAIN_ONE + 1, :]
    pre_ref[...] = dot(xpad_ref[...], w_ref[...])

    def body(i, _):
        normed = (pre_ref[row_at(i), :] - center) * scale
        grad = factor * (grad_ref[row_at(i), :] - mean_first - normed * mean_second)
        gpe_ref[row_at(i), lanes_at(step)] = jnp.where(mask, grad, 0.0).astype(BF16)
        return 0

    each_row(body, 0)
    base = pl.multiple_of(step * LATE, 16)
    grads_ref[pl.ds(base, C), :] = dot(xturn_ref[...], gpe_ref[:, lanes_at(step)])
    grads_ref[pl.ds(pl.multiple_of(base + C, 16), TABLE), :] = sums_ref[...]

    @pl.when(step == CHUNKS - 1)
    def _():
        grads_ref[CHUNKS * LATE :, :] = jnp.zeros((LATE_ROWS - CHUNKS * LATE, LANES), F32)
        acc_ref[...] = cpad_ref[...].astype(F32) + dot(gpe_ref[...], wturn_ref[...])
        for i in range(SIDE):
            out_ref[i] = acc_ref[i * WIDE : i * WIDE + SIDE, :].astype(BF16)


def put_row(ref, rows_ref, row, height, scale):
    for c in range(-(-ref.shape[1] // LANES)):
        width = min(LANES, ref.shape[1] - c * LANES)
        at = c * height + row
        ref[:, c * LANES : c * LANES + width] = rows_ref[at : at + ref.shape[0], 0:width] * scale


def unpack_early_kernel(
    scale,
    rows_ref,
    project_ref,
    restore_ref,
    reduce_ref,
    brestore_ref,
    shift_ref,
    gain_ref,
    gproject_ref,
    breduce_ref,
    upper_ref,
):
    put_row(project_ref, rows_ref, 0, EARLY, scale)
    put_row(restore_ref, rows_ref, C, EARLY, scale)
    put_row(reduce_ref, rows_ref, C + SE_ROWS, EARLY, scale)
    put_row(brestore_ref, rows_ref, C + SE, EARLY, scale)
    put_row(shift_ref, rows_ref, C + SE + 1, EARLY, scale)
    put_row(gain_ref, rows_ref, C + SE + 2, EARLY, scale)
    put_row(gproject_ref, rows_ref, C + SE + 3, EARLY, scale)
    at = 2 * EARLY + C + SE + 3
    breduce_ref[...] = rows_ref[at : at + 1, 0:SE] * scale
    upper_ref[...] = rows_ref[UPPER_AT : UPPER_AT + UPPER_ROWS, :]


def unpack_late_kernel(scale, rows_ref, expand_ref, depth_ref, shift_ref, gain_ref):
    put_row(expand_ref, rows_ref, 0, LATE, scale)
    put_row(depth_ref, rows_ref, C, LATE, scale)
    put_row(shift_ref, rows_ref, C + 25, LATE, scale)
    put_row(gain_ref, rows_ref, C + 26, LATE, scale)


def unpack(kernel, rows, shapes, scale):
    return pl.pallas_call(
        functools.partial(kernel, scale),
        out_shape=tuple(f32(*shape) for shape in shapes),
        compiler_params=pltpu.CompilerParams(vmem_limit_bytes=20 * 2**20),
        cost_estimate=pl.CostEstimate(
            flops=rows.size, bytes_accessed=8 * rows.size, transcendentals=0
        ),
    )(rows)


def whole(shape):
    return pl.BlockSpec(shape, lambda c: (0,) * len(shape))


def lane_block(rows):
    return pl.BlockSpec((rows, LANES), lambda c: (0, c))


def peer_block(peers):
    return pl.BlockSpec((peers, 2, LANES), lambda c: (0, 0, c))


MAP_BLOCK = pl.BlockSpec((pl.squeezed, ROWS, LANES), lambda c: (c, 0, 0))
MAP = jax.ShapeDtypeStruct((CHUNKS, ROWS, LANES), F32)
MAP_BF16 = jax.ShapeDtypeStruct((CHUNKS, ROWS, LANES), BF16)
EDGE = jax.ShapeDtypeStruct((ROWS, C), F32)
EDGE_BF16 = jax.ShapeDtypeStruct((ROWS, C), BF16)


def f32(*shape):
    return jax.ShapeDtypeStruct(shape, F32)


def call(kernel, ins, outs, scratch, flops):
    return pl.pallas_call(
        kernel,
        grid=(CHUNKS,),
        in_specs=ins,
        out_specs=tuple(spec for spec, _ in outs),
        out_shape=tuple(shape for _, shape in outs),
        scratch_shapes=scratch,
        compiler_params=pltpu.CompilerParams(vmem_limit_bytes=20 * 2**20),
        cost_estimate=pl.CostEstimate(
            flops=flops, bytes_accessed=12 * 2**20, transcendentals=ROWS * PADDED
        ),
    )


def exchange(copies, axes):
    return lax.all_to_all(copies, axes, 0, 0, tiled=True)


def swap(rows):
    return lax.ppermute(rows, "core", [(i, i ^ 1) for i in range(lax.axis_size("core"))])


def pair_sum(rows):
    chips = lax.axis_size(CHIPS)
    near = lax.axis_index("core") == 0
    halves = rows.reshape(2, chips, -1, PIECE, LANES)
    mine = jnp.where(near, halves[0], halves[1])
    return mine + swap(jnp.where(near, halves[1], halves[0]))


def chip_sum(mine):
    return jnp.sum(exchange(mine, CHIPS), axis=0)


def all_parts(mine):
    chips = lax.axis_size(CHIPS)
    near = lax.axis_index("core") == 0
    half = exchange(jnp.broadcast_to(mine[None], (chips,) + mine.shape), CHIPS)
    other = swap(half)
    return jnp.stack([jnp.where(near, half, other), jnp.where(near, other, half)])


def tie(first, second):
    return lax.optimization_barrier((first, second))


def per_device(
    block_input,
    cotangent,
    w_expand,
    gain_expand,
    shift_expand,
    w_depth,
    gain_depth,
    shift_depth,
    w_reduce,
    b_reduce,
    w_restore,
    b_restore,
    w_project,
    gain_project,
    upper_grads,
):
    peers = lax.axis_size(GROUP)
    images_total = lax.axis_size(AXES)
    extra = PADDED - HID
    images, cot = block_input[0, 0], cotangent[0, 0]
    wexp = jnp.pad(w_expand, ((0, 0), (0, extra)))
    wproj = jnp.pad(w_project, ((0, extra), (0, 0)))
    wproj_turn = jnp.pad(w_project.T, ((0, 0), (0, extra)))
    wexp_turn = jnp.pad(w_expand.T, ((0, extra), (0, 0)))
    wred = jnp.pad(w_reduce.astype(F32).T, ((0, SE_ROWS - SE), (0, extra)))
    wres = jnp.pad(w_restore.astype(F32), ((0, SE_ROWS - SE), (0, extra)))
    bred = jnp.broadcast_to(jnp.pad(b_reduce, (0, SE_ROWS - SE))[:, None], (SE_ROWS, LANES))
    bres = jnp.pad(b_restore, (0, extra))[None]
    table = jnp.concatenate(
        [w_depth.astype(F32)]
        + [v[None] for v in (gain_expand, shift_expand, gain_depth, shift_depth)],
        axis=0,
    )
    table = jnp.pad(table, ((0, TABLE - table.shape[0]), (0, extra)))
    xpad_spec, w_spec = whole((ROWS, C)), lane_block(C)
    se_spec = whole((SE_ROWS, PADDED))
    stat_out = (peer_block(peers), f32(peers, 2, PADDED))
    stat_whole = (whole((peers, 2, PADDED)), f32(peers, 2, PADDED))
    moments = (lane_block(8), f32(8, PADDED))
    map_f32 = pltpu.VMEM((ROWS, LANES), F32)
    map_bf16 = pltpu.VMEM((ROWS, LANES), BF16)
    line = pltpu.VMEM((2, WIDE, C), F32)
    taps = pltpu.VMEM((KER * KER * 8, LANES), F32)
    halo = pltpu.VMEM((HALO, LANES), F32)
    matmul = 2 * ROWS * C * PADDED

    xpad, stat = call(
        stats_kernel,
        [whole((SIDE, SIDE, C)), w_spec],
        [(xpad_spec, EDGE_BF16), stat_out],
        [map_f32, line],
        matmul,
    )(images, wexp)
    gathered = exchange(stat, GROUP)
    depth, stat, moment_one = call(
        forward_kernel,
        [xpad_spec, w_spec, peer_block(peers), lane_block(TABLE)],
        [(MAP_BLOCK, MAP), stat_out, moments],
        [map_f32, halo, taps],
        50 * ROWS * PADDED,
    )(xpad, wexp, gathered, table)
    gathered = exchange(stat, GROUP)
    moment_two, project, cpad, vector, column, stat = call(
        project_kernel,
        [
            MAP_BLOCK,
            peer_block(peers),
            lane_block(TABLE),
            whole((PADDED, C)),
            whole((SIDE, SIDE, C)),
            se_spec,
            se_spec,
            whole((SE_ROWS, LANES)),
            whole((1, PADDED)),
        ],
        [
            moments,
            (whole((ROWS, C)), EDGE),
            (whole((ROWS, C)), EDGE_BF16),
            (whole((8, PADDED)), f32(8, PADDED)),
            (whole((2, SE_ROWS, LANES)), f32(2, SE_ROWS, LANES)),
            (whole((peers, 4, C)), f32(peers, 4, C)),
        ],
        [
            pltpu.VMEM((CHUNKS, ROWS, LANES), BF16),
            pltpu.VMEM((ROWS, PADDED), BF16),
            line,
        ],
        matmul,
    )(depth, gathered, table, wproj, cot, wred, wres, bred, bres)
    gathered = exchange(stat, GROUP)
    first, slope, hidden, gpp, rows, reduce, stat = call(
        back_project_kernel,
        [
            MAP_BLOCK,
            whole((peers, 4, C)),
            lane_block(TABLE),
            lane_block(8),
            whole((ROWS, C)),
            whole((ROWS, C)),
            whole((1, C)),
            w_spec,
            whole((8, PADDED)),
            whole((2, SE_ROWS, LANES)),
            se_spec,
            se_spec,
        ],
        [
            (MAP_BLOCK, MAP),
            (MAP_BLOCK, MAP),
            (MAP_BLOCK, MAP_BF16),
            (whole((ROWS, C)), EDGE_BF16),
            (whole((8, PADDED)), f32(8, PADDED)),
            (whole((SE_ROWS, LANES)), f32(SE_ROWS, LANES)),
            stat_whole,
        ],
        [map_f32, pltpu.VMEM((8, PADDED), F32)],
        2 * matmul,
    )(
        depth,
        gathered,
        table,
        moment_two,
        project,
        cpad,
        gain_project[None],
        wproj_turn,
        vector,
        column,
        wred,
        wres,
    )
    gathered = exchange(stat, GROUP)
    (early,) = call(
        early_kernel,
        [
            whole((ROWS, C)),
            MAP_BLOCK,
            lane_block(8),
            whole((SE_ROWS, LANES)),
            lane_block(8),
            whole((2, SE_ROWS, LANES)),
            whole((UPPER_ROWS, LANES)),
        ],
        [(whole((EARLY_ROWS, LANES)), f32(EARLY_ROWS, LANES))],
        [],
        10 * matmul,
    )(gpp, hidden, rows, reduce, vector, column, upper_grads[0].reshape(-1, LANES))
    early, gathered = tie(pair_sum(early), gathered)
    early = chip_sum(early)
    grad_one, stat, sums, field, back = call(
        back_depth_kernel,
        [
            MAP_BLOCK,
            MAP_BLOCK,
            MAP_BLOCK,
            peer_block(peers),
            lane_block(TABLE),
            lane_block(8),
            lane_block(8),
            lane_block(8),
            lane_block(8),
            xpad_spec,
            w_spec,
        ],
        [
            (MAP_BLOCK, MAP),
            stat_out,
            (lane_block(8), f32(8, PADDED)),
            (MAP_BLOCK, MAP_BF16),
            (MAP_BLOCK, MAP),
        ],
        [map_f32, halo, map_f32, taps],
        100 * ROWS * PADDED,
    )(depth, first, slope, gathered, table, moment_two, moment_one, vector, rows, xpad, wexp)
    stat, early, field = lax.optimization_barrier((stat, early, field))
    gathered = exchange(stat, GROUP)
    (sums,) = call(
        kernel_grad_kernel,
        [MAP_BLOCK, MAP_BLOCK, lane_block(8)],
        [(lane_block(TABLE), f32(TABLE, PADDED))],
        [halo],
        50 * ROWS * PADDED,
    )(field, back, sums)
    input_grad, late = call(
        back_expand_kernel,
        [
            MAP_BLOCK,
            peer_block(peers),
            lane_block(TABLE),
            lane_block(8),
            xpad_spec,
            w_spec,
            lane_block(TABLE),
            xpad_spec,
            whole((C, ROWS)),
            whole((PADDED, C)),
        ],
        [
            (whole((SIDE, SIDE, C)), jax.ShapeDtypeStruct((SIDE, SIDE, C), BF16)),
            (whole((LATE_ROWS, LANES)), f32(LATE_ROWS, LANES)),
        ],
        [map_f32, pltpu.VMEM((ROWS, PADDED), BF16), pltpu.VMEM((ROWS, C), F32)],
        3 * matmul,
    )(grad_one, gathered, table, moment_one, xpad, wexp, sums, cpad, xpad.T, wexp_turn)

    late = chip_sum(pair_sum(late))
    split = early.shape[0]
    full = all_parts(jnp.concatenate([early, late]))
    early = full[:, :, :split].reshape(EARLY_ROWS, LANES)
    late = full[:, :, split:].reshape(LATE_ROWS, LANES)

    scale = 1.0 / images_total
    wide = (1, HID)
    g_project, g_restore, g_reduce, g_brestore, g_shift_two, g_gain_two, g_gproject, g_breduce, upper = (
        unpack(
            unpack_early_kernel,
            early,
            [(C, HID), (SE, HID), (SE, HID), wide, wide, wide, (1, C), (1, SE), (UPPER_ROWS, LANES)],
            scale,
        )
    )
    g_expand, g_depth, g_shift_one, g_gain_one = unpack(
        unpack_late_kernel, late, [(C, HID), (KER * KER, HID), wide, wide], scale
    )
    return (
        input_grad[None, None],
        g_expand,
        g_gain_one[0],
        g_shift_one[0],
        g_depth,
        g_gain_two[0],
        g_shift_two[0],
        g_reduce.T,
        g_breduce[0],
        g_restore,
        g_brestore[0],
        g_project.T,
        g_gproject[0],
        upper.reshape(-1),
    )


def solution(mesh):
    chips = Mesh(mesh.devices.reshape(SHAPE), AXES)
    maps = P(("z", "core"), GROUP, None, None, None)
    return jax.shard_map(
        per_device,
        mesh=chips,
        in_specs=(maps, maps) + (P(),) * 12 + (P(AXES, None),),
        out_specs=(maps,) + (P(),) * 13,
        check_vma=False,
    )
```

```python
import functools

import jax
import jax.numpy as jnp
from jax import lax
from jax.experimental import pallas as pl
from jax.experimental.pallas import tpu as pltpu
from jax.sharding import Mesh, PartitionSpec as P

KER = 5
EPSILON = 0.001
SHAPE = (4, 8, 8, 2)
AXES = ("x", "y", "z", "core")
GROUP = ("x", "y")
PLANE = ("y", "z")
SIDE = 29
WIDE = 32
ROWS = SIDE * WIDE
HALO = (SIDE + KER - 1) * WIDE
C = 176
HID = 1056
LANES = 128
CHUNKS = 9
PADDED = CHUNKS * LANES
SE = 44
SE_ROWS = 48
SPOTS = SIDE * SIDE
GAIN_ONE, SHIFT_ONE, GAIN_TWO, SHIFT_TWO, BIAS = 25, 26, 27, 28, 29
TABLE = 32
EARLY = C + 2 * SE_ROWS
UPPER_AT = CHUNKS * EARLY
UPPER_ROWS = 1024
EARLY_ROWS = 4096
LATE = C + TABLE
LATE_ROWS = 2048
F32 = jnp.float32
BF16 = jnp.bfloat16


def dot(left, right, left_dim=1, right_dim=0):
    return lax.dot_general(
        left, right, (((left_dim,), (right_dim,)), ((), ())), preferred_element_type=F32
    )


def logistic(values):
    return 0.5 + 0.5 * jnp.tanh(0.5 * values)


def valid_mask(lanes=LANES):
    return lax.broadcasted_iota(jnp.int32, (WIDE, lanes), 0) < SIDE


def row_at(index):
    if isinstance(index, int):
        return slice(index * WIDE, (index + 1) * WIDE)
    return pl.ds(pl.multiple_of(index * WIDE, WIDE), WIDE)


def each_row(body, init):
    for i in range(SIDE):
        init = body(i, init)
    return init


def loop_rows(body, init):
    return lax.fori_loop(0, SIDE, body, init)


def col_sum(values):
    return jnp.sum(values, axis=0, keepdims=True)


def zeros(lanes=LANES):
    return jnp.zeros((WIDE, lanes), F32)


def share(pair, ref):
    ref[...] = jnp.broadcast_to(pair[None], ref.shape)


def pair_rows(first, second):
    return jnp.where(lax.broadcasted_iota(jnp.int32, (2, first.shape[1]), 0) == 0, first, second)


def spread_of(ref, mean, mask):
    def body(i, acc):
        dev = jnp.where(mask, ref[row_at(i), :] - mean, 0.0)
        return acc + dev * dev

    return col_sum(each_row(body, zeros(mean.shape[1]))) / SPOTS


def merged(gathered):
    peers = gathered.shape[0]
    total = jnp.sum(gathered, axis=0)
    center = total[0:1] / peers
    dev = jnp.sum(jnp.square(gathered[:, 0:1, :] - center[None]), axis=0)
    spread = (total[1:2] + dev) / peers
    return center, lax.rsqrt(spread + EPSILON)


def widen(map_ref, flat_ref, line_ref):
    line_ref[...] = jnp.zeros_like(line_ref)
    for i in range(SIDE):
        line_ref[i % 2, 0:SIDE, :] = map_ref[i].astype(F32)
        flat_ref[i * WIDE : (i + 1) * WIDE, :] = line_ref[i % 2].astype(BF16)


def stats_kernel(x_ref, w_ref, xpad_ref, stat_ref, pre_ref, line_ref):
    @pl.when(pl.program_id(0) == 0)
    def _():
        widen(x_ref, xpad_ref, line_ref)

    pre_ref[...] = dot(xpad_ref[...], w_ref[...])
    total = each_row(lambda i, acc: acc + pre_ref[row_at(i), :], zeros())
    mean = col_sum(total) / SPOTS
    share(pair_rows(mean, spread_of(pre_ref, mean, valid_mask())), stat_ref)


def slide(parts, sign):
    out = parts[2]
    for b in (0, 1, 3, 4):
        out = out + pltpu.roll(parts[b], (sign * (2 - b)) % WIDE, 0)
    return out


def row_taps(halo_ref, tap_ref, i, flip):
    parts = [None] * KER
    for a in range(KER):
        source = halo_ref[row_at(i + a), :].reshape(WIDE // 8, 8, LANES)
        for b in range(KER):
            k = ((KER - 1 - a) if flip else a) * KER + b
            term = source * tap_ref[k * 8 : k * 8 + 8, :]
            parts[b] = term if parts[b] is None else parts[b] + term
    return slide([part.reshape(WIDE, LANES) for part in parts], -1 if flip else 1)


def clear_halo(ref):
    edge = jnp.zeros((2 * WIDE, LANES), F32)
    ref[0 : 2 * WIDE, :] = edge
    ref[HALO - 2 * WIDE : HALO, :] = edge


def spread_taps(table_ref, tap_ref):
    for k in range(KER * KER):
        tap_ref[k * 8 : k * 8 + 8, :] = jnp.broadcast_to(table_ref[k : k + 1, :], (8, LANES))


def forward_kernel(
    xpad_ref,
    w_ref,
    gathered_ref,
    table_ref,
    depth_ref,
    stat_ref,
    moment_ref,
    pre_ref,
    halo_ref,
    tap_ref,
):
    @pl.when(pl.program_id(0) == 0)
    def _():
        clear_halo(halo_ref)

    mask = valid_mask()
    center, scale = merged(gathered_ref[...])
    moment_ref[0:1, :] = center
    moment_ref[1:2, :] = scale
    slope = scale * table_ref[GAIN_ONE : GAIN_ONE + 1, :]
    offset = table_ref[SHIFT_ONE : SHIFT_ONE + 1, :] - center * slope
    pre_ref[...] = dot(xpad_ref[...], w_ref[...])

    def activate(i, _):
        act = pre_ref[row_at(i), :] * slope + offset
        silu = (act * logistic(act)).astype(BF16).astype(F32)
        halo_ref[row_at(i + 2), :] = jnp.where(mask, silu, 0.0)
        return 0

    each_row(activate, 0)
    spread_taps(table_ref, tap_ref)

    def filter_row(i, acc):
        out = jnp.where(mask, row_taps(halo_ref, tap_ref, i, False), 0.0)
        depth_ref[row_at(i), :] = out
        return acc + out

    mean = col_sum(loop_rows(filter_row, zeros())) / SPOTS
    share(pair_rows(mean, spread_of(depth_ref, mean, mask)), stat_ref)


def lanes_at(index):
    return pl.ds(pl.multiple_of(index * LANES, LANES), LANES)


def project_kernel(
    depth_ref,
    gathered_ref,
    table_ref,
    wproject_ref,
    cot_ref,
    wreduce_ref,
    wrestore_ref,
    breduce_ref,
    brestore_ref,
    moment_ref,
    project_ref,
    cpad_ref,
    vector_ref,
    column_ref,
    stat_ref,
    act_ref,
    hidden_ref,
    line_ref,
):
    step = pl.program_id(0)
    mask = valid_mask()
    center, scale = merged(gathered_ref[...])
    moment_ref[0:1, :] = center
    moment_ref[1:2, :] = scale
    slope = scale * table_ref[GAIN_TWO : GAIN_TWO + 1, :]
    offset = table_ref[SHIFT_TWO : SHIFT_TWO + 1, :] - center * slope

    def activate(i, acc):
        act = depth_ref[row_at(i), :] * slope + offset
        silu = jnp.where(mask, act * logistic(act), 0.0).astype(BF16)
        act_ref[step, row_at(i), :] = silu
        return acc + silu.astype(F32)

    vector_ref[0:1, lanes_at(step)] = col_sum(each_row(activate, zeros())) / SPOTS

    @pl.when(step == 0)
    def _():
        widen(cot_ref, cpad_ref, line_ref)

    @pl.when(step == CHUNKS - 1)
    def _():
        pooled = vector_ref[0:1, :]
        logit = jnp.sum(wreduce_ref[...] * pooled, axis=1, keepdims=True) + breduce_ref[...]
        squeezed = logit * logistic(logit)
        column_ref[0] = logit
        column_ref[1] = squeezed
        restored = col_sum(wrestore_ref[...] * squeezed[:, 0:1]) + brestore_ref[...]
        vector_ref[1:2, :] = logistic(restored)

        def fill(c, _):
            excite = vector_ref[1:2, lanes_at(c)]

            def scale_row(i, _):
                hidden_ref[row_at(i), lanes_at(c)] = (
                    act_ref[c, row_at(i), :].astype(F32) * excite
                ).astype(BF16)
                return 0

            each_row(scale_row, 0)
            return 0

        lax.fori_loop(0, CHUNKS, fill, 0)
        project_ref[...] = dot(hidden_ref[...], wproject_ref[...])

        def sums(i, accs):
            values, incoming = project_ref[row_at(i), :], cpad_ref[row_at(i), :].astype(F32)
            return accs[0] + values, accs[1] + incoming

        total, cot_total = each_row(sums, (zeros(C), zeros(C)))
        mean = col_sum(total) / SPOTS

        def devs(i, accs):
            dev = jnp.where(valid_mask(C), project_ref[row_at(i), :] - mean, 0.0)
            incoming = cpad_ref[row_at(i), :].astype(F32)
            return accs[0] + dev * dev, accs[1] + incoming * dev

        square, cross = each_row(devs, (zeros(C), zeros(C)))
        row = lax.broadcasted_iota(jnp.int32, (4, C), 0)
        packed = jnp.where(
            row == 0,
            mean,
            jnp.where(
                row == 1,
                col_sum(square) / SPOTS,
                jnp.where(row == 2, col_sum(cot_total), col_sum(cross)),
            ),
        )
        share(packed, stat_ref)


def back_project_kernel(
    depth_ref,
    gathered_ref,
    table_ref,
    moment_ref,
    project_ref,
    cpad_ref,
    gain_ref,
    wproject_ref,
    vector_ref,
    column_ref,
    wreduce_ref,
    wrestore_ref,
    first_ref,
    slope_ref,
    hidden_ref,
    gpp_ref,
    row_ref,
    reduce_ref,
    stat_ref,
    back_ref,
    sums_ref,
):
    step = pl.program_id(0)
    mask = valid_mask()

    @pl.when(step == 0)
    def _():
        gathered = gathered_ref[...]
        peers = gathered.shape[0]
        count = peers * SPOTS
        total = jnp.sum(gathered, axis=0)
        center3 = total[0:1] / peers
        away = gathered[:, 0:1, :] - center3[None]
        spread = (total[1:2] + jnp.sum(jnp.square(away), axis=0)) / peers
        scale3 = lax.rsqrt(spread + EPSILON)
        cross = total[3:4] + jnp.sum(gathered[:, 2:3, :] * away, axis=0)
        first = total[2:3] / count
        second = cross * scale3 / count
        factor = scale3 * gain_ref[...]
        wide = valid_mask(C)

        def body(i, acc):
            normed = (project_ref[row_at(i), :] - center3) * scale3
            incoming = cpad_ref[row_at(i), :].astype(F32)
            grad = factor * (incoming - first - normed * second)
            gpp_ref[row_at(i), :] = jnp.where(wide, grad, 0.0).astype(BF16)
            return acc + incoming * normed

        row_ref[...] = jnp.zeros_like(row_ref)
        row_ref[4:5, 0:C] = col_sum(each_row(body, zeros(C)))

    center, scale = moment_ref[0:1, :], moment_ref[1:2, :]
    gain = table_ref[GAIN_TWO : GAIN_TWO + 1, :]
    shift = table_ref[SHIFT_TWO : SHIFT_TWO + 1, :]
    excite = vector_ref[1:2, lanes_at(step)]
    back_ref[...] = dot(gpp_ref[...], wproject_ref[...])

    def body(i, accs):
        normed = (depth_ref[row_at(i), :] - center) * scale
        act = normed * gain + shift
        sig = logistic(act)
        silu = (act * sig).astype(BF16).astype(F32)
        slope = jnp.where(mask, sig * (1.0 + act * (1.0 - sig)), 0.0)
        hidden_ref[row_at(i), :] = jnp.where(mask, silu * excite, 0.0).astype(BF16)
        back = back_ref[row_at(i), :]
        first = back * slope
        first_ref[row_at(i), :] = first
        slope_ref[row_at(i), :] = slope
        return (
            accs[0] + back * silu,
            accs[1] + first,
            accs[2] + first * normed,
            accs[3] + slope,
            accs[4] + slope * normed,
        )

    totals = each_row(body, tuple(zeros() for _ in range(5)))
    for k in range(5):
        sums_ref[k : k + 1, lanes_at(step)] = col_sum(totals[k])

    @pl.when(step == CHUNKS - 1)
    def _():
        excite = vector_ref[1:2, :]
        logit = column_ref[0]
        grad_logit = sums_ref[0:1, :] * excite * (1.0 - excite)
        grad_squeezed = jnp.sum(wrestore_ref[...] * grad_logit, axis=1, keepdims=True)
        sig = logistic(logit)
        grad_reduce = grad_squeezed * (sig * (1.0 + logit * (1.0 - sig)))
        grad_pooled = col_sum(wreduce_ref[...] * grad_reduce[:, 0:1]) / SPOTS
        shift_sum = excite * sums_ref[1:2, :] + grad_pooled * sums_ref[3:4, :]
        gain_sum = excite * sums_ref[2:3, :] + grad_pooled * sums_ref[4:5, :]
        share(pair_rows(shift_sum, gain_sum), stat_ref)
        row_ref[0:1, :] = grad_pooled
        row_ref[1:2, :] = grad_logit
        row_ref[2:3, :] = shift_sum
        row_ref[3:4, :] = gain_sum
        reduce_ref[...] = grad_reduce


def early_kernel(
    gpp_ref, hidden_ref, row_ref, reduce_ref, vector_ref, column_ref, upper_ref, grads_ref
):
    step = pl.program_id(0)
    base = pl.multiple_of(step * EARLY, 16)
    grads_ref[pl.ds(base, C), :] = dot(gpp_ref[...], hidden_ref[...], 0, 0)
    lane = lax.broadcasted_iota(jnp.int32, (SE_ROWS, LANES), 1)
    row = lax.broadcasted_iota(jnp.int32, (SE_ROWS, LANES), 0)
    squeezed, grad_reduce = column_ref[1], reduce_ref[...]
    block = squeezed * row_ref[1:2, :]
    block = jnp.where(row == SE, row_ref[1:2, :], block)
    block = jnp.where(row == SE + 1, row_ref[2:3, :], block)
    block = jnp.where(row == SE + 2, row_ref[3:4, :], block)
    bias_row = col_sum(jnp.where(lane == row, grad_reduce, 0.0))
    extra = jnp.where(step < 2, row_ref[4:5, :], bias_row)
    block = jnp.where(row == SE + 3, extra, block)
    grads_ref[pl.ds(pl.multiple_of(base + C, 16), SE_ROWS), :] = block
    grads_ref[pl.ds(pl.multiple_of(base + C + SE_ROWS, 16), SE_ROWS), :] = (
        grad_reduce * vector_ref[0:1, :]
    )

    @pl.when(step == 0)
    def _():
        grads_ref[UPPER_AT : UPPER_AT + UPPER_ROWS, :] = upper_ref[...]
        rest = EARLY_ROWS - UPPER_AT - UPPER_ROWS
        grads_ref[UPPER_AT + UPPER_ROWS :, :] = jnp.zeros((rest, LANES), F32)


def back_depth_kernel(
    depth_ref,
    first_ref,
    slope_ref,
    gathered_ref,
    table_ref,
    moment_two_ref,
    moment_one_ref,
    vector_ref,
    pooled_ref,
    xpad_ref,
    w_ref,
    grad_ref,
    stat_ref,
    sums_ref,
    field_ref,
    back_ref,
    pre_ref,
    ghalo_ref,
    side_ref,
    tap_ref,
):
    @pl.when(pl.program_id(0) == 0)
    def _():
        clear_halo(ghalo_ref)

    mask = valid_mask()
    total = jnp.sum(gathered_ref[...], axis=0)
    gain = table_ref[GAIN_TWO : GAIN_TWO + 1, :]
    count = gathered_ref.shape[0] * SPOTS
    mean_first = gain * total[0:1] / count
    mean_second = gain * total[1:2] / count
    center, scale = moment_two_ref[0:1, :], moment_two_ref[1:2, :]
    excite = vector_ref[1:2, :] * gain
    pooled = pooled_ref[0:1, :] * gain
    center_one, scale_one = moment_one_ref[0:1, :], moment_one_ref[1:2, :]
    slope_one = scale_one * table_ref[GAIN_ONE : GAIN_ONE + 1, :]
    offset_one = table_ref[SHIFT_ONE : SHIFT_ONE + 1, :] - center_one * slope_one
    pre_ref[...] = dot(xpad_ref[...], w_ref[...])

    def prepare(i, _):
        normed = (depth_ref[row_at(i), :] - center) * scale
        grad = first_ref[row_at(i), :] * excite + slope_ref[row_at(i), :] * pooled
        grad = jnp.where(mask, scale * (grad - mean_first - normed * mean_second), 0.0)
        ghalo_ref[row_at(i + 2), :] = grad
        back_ref[row_at(i), :] = grad
        act = pre_ref[row_at(i), :] * slope_one + offset_one
        sig = logistic(act)
        field_ref[row_at(i), :] = jnp.where(mask, act * sig, 0.0).astype(BF16)
        side_ref[row_at(i), :] = jnp.where(mask, sig * (1.0 + act * (1.0 - sig)), 0.0)
        return 0

    each_row(prepare, 0)
    spread_taps(table_ref, tap_ref)

    def input_grad(i, accs):
        grad = row_taps(ghalo_ref, tap_ref, i, True) * side_ref[row_at(i), :]
        grad_ref[row_at(i), :] = grad
        normed = (pre_ref[row_at(i), :] - center_one) * scale_one
        return accs[0] + grad, accs[1] + grad * normed

    shift_sum, gain_sum = (col_sum(a) for a in loop_rows(input_grad, (zeros(), zeros())))
    share(pair_rows(shift_sum, gain_sum), stat_ref)
    sums_ref[...] = jnp.zeros_like(sums_ref)
    sums_ref[0:1, :] = shift_sum
    sums_ref[1:2, :] = gain_sum


def kernel_grad_kernel(field_ref, back_ref, sums_ref, out_ref, halo_ref):
    @pl.when(pl.program_id(0) == 0)
    def _():
        clear_halo(halo_ref)

    halo_ref[2 * WIDE : 2 * WIDE + ROWS, :] = field_ref[...].astype(F32)

    def kernel_grad(i, accs):
        grad = back_ref[row_at(i), :]
        shifted = [
            (grad if b == 2 else pltpu.roll(grad, (b - 2) % WIDE, 0)).reshape(
                WIDE // 8, 8, LANES
            )
            for b in range(KER)
        ]
        accs = list(accs)
        for a in range(KER):
            field = halo_ref[row_at(i + a), :].reshape(WIDE // 8, 8, LANES)
            for b in range(KER):
                accs[a * KER + b] = accs[a * KER + b] + jnp.sum(field * shifted[b], axis=0)
        return tuple(accs)

    start = tuple(jnp.zeros((8, LANES), F32) for _ in range(KER * KER))
    accs = loop_rows(kernel_grad, start)
    for k in range(KER * KER):
        out_ref[k : k + 1, :] = col_sum(accs[k])
    out_ref[25:TABLE, :] = sums_ref[0 : TABLE - 25, :]


def back_expand_kernel(
    grad_ref,
    gathered_ref,
    table_ref,
    moment_ref,
    xpad_ref,
    w_ref,
    sums_ref,
    cpad_ref,
    xturn_ref,
    wturn_ref,
    out_ref,
    grads_ref,
    pre_ref,
    gpe_ref,
    acc_ref,
):
    step = pl.program_id(0)
    mask = valid_mask()
    total = jnp.sum(gathered_ref[...], axis=0)
    count = gathered_ref.shape[0] * SPOTS
    mean_first, mean_second = total[0:1] / count, total[1:2] / count
    center, scale = moment_ref[0:1, :], moment_ref[1:2, :]
    factor = scale * table_ref[GAIN_ONE : GAIN_ONE + 1, :]
    pre_ref[...] = dot(xpad_ref[...], w_ref[...])

    def body(i, _):
        normed = (pre_ref[row_at(i), :] - center) * scale
        grad = factor * (grad_ref[row_at(i), :] - mean_first - normed * mean_second)
        gpe_ref[row_at(i), lanes_at(step)] = jnp.where(mask, grad, 0.0).astype(BF16)
        return 0

    each_row(body, 0)
    base = pl.multiple_of(step * LATE, 16)
    grads_ref[pl.ds(base, C), :] = dot(xturn_ref[...], gpe_ref[:, lanes_at(step)])
    grads_ref[pl.ds(pl.multiple_of(base + C, 16), TABLE), :] = sums_ref[...]

    @pl.when(step == CHUNKS - 1)
    def _():
        grads_ref[CHUNKS * LATE :, :] = jnp.zeros((LATE_ROWS - CHUNKS * LATE, LANES), F32)
        acc_ref[...] = cpad_ref[...].astype(F32) + dot(gpe_ref[...], wturn_ref[...])
        for i in range(SIDE):
            out_ref[i] = acc_ref[i * WIDE : i * WIDE + SIDE, :].astype(BF16)


def put_row(ref, rows_ref, row, height, scale):
    for c in range(-(-ref.shape[1] // LANES)):
        width = min(LANES, ref.shape[1] - c * LANES)
        at = c * height + row
        ref[:, c * LANES : c * LANES + width] = rows_ref[at : at + ref.shape[0], 0:width] * scale


def unpack_early_kernel(
    scale,
    rows_ref,
    project_ref,
    restore_ref,
    reduce_ref,
    brestore_ref,
    shift_ref,
    gain_ref,
    gproject_ref,
    breduce_ref,
    upper_ref,
):
    put_row(project_ref, rows_ref, 0, EARLY, scale)
    put_row(restore_ref, rows_ref, C, EARLY, scale)
    put_row(reduce_ref, rows_ref, C + SE_ROWS, EARLY, scale)
    put_row(brestore_ref, rows_ref, C + SE, EARLY, scale)
    put_row(shift_ref, rows_ref, C + SE + 1, EARLY, scale)
    put_row(gain_ref, rows_ref, C + SE + 2, EARLY, scale)
    put_row(gproject_ref, rows_ref, C + SE + 3, EARLY, scale)
    at = 2 * EARLY + C + SE + 3
    breduce_ref[...] = rows_ref[at : at + 1, 0:SE] * scale
    upper_ref[...] = rows_ref[UPPER_AT : UPPER_AT + UPPER_ROWS, :]


def unpack_late_kernel(scale, rows_ref, expand_ref, depth_ref, shift_ref, gain_ref):
    put_row(expand_ref, rows_ref, 0, LATE, scale)
    put_row(depth_ref, rows_ref, C, LATE, scale)
    put_row(shift_ref, rows_ref, C + 25, LATE, scale)
    put_row(gain_ref, rows_ref, C + 26, LATE, scale)


def unpack(kernel, rows, shapes, scale):
    return pl.pallas_call(
        functools.partial(kernel, scale),
        out_shape=tuple(f32(*shape) for shape in shapes),
        compiler_params=pltpu.CompilerParams(vmem_limit_bytes=56 * 2**20),
        cost_estimate=pl.CostEstimate(
            flops=rows.size, bytes_accessed=8 * rows.size, transcendentals=0
        ),
    )(rows)


def whole(shape):
    return pl.BlockSpec(shape, lambda c: (0,) * len(shape))


def lane_block(rows):
    return pl.BlockSpec((rows, LANES), lambda c: (0, c))


def peer_block(peers):
    return pl.BlockSpec((peers, 2, LANES), lambda c: (0, 0, c))


MAP_BLOCK = pl.BlockSpec((pl.squeezed, ROWS, LANES), lambda c: (c, 0, 0))
MAP = jax.ShapeDtypeStruct((CHUNKS, ROWS, LANES), F32)
MAP_BF16 = jax.ShapeDtypeStruct((CHUNKS, ROWS, LANES), BF16)
EDGE = jax.ShapeDtypeStruct((ROWS, C), F32)
EDGE_BF16 = jax.ShapeDtypeStruct((ROWS, C), BF16)


def f32(*shape):
    return jax.ShapeDtypeStruct(shape, F32)


def call(kernel, ins, outs, scratch, flops):
    return pl.pallas_call(
        kernel,
        grid=(CHUNKS,),
        in_specs=ins,
        out_specs=tuple(spec for spec, _ in outs),
        out_shape=tuple(shape for _, shape in outs),
        scratch_shapes=scratch,
        compiler_params=pltpu.CompilerParams(vmem_limit_bytes=56 * 2**20),
        cost_estimate=pl.CostEstimate(
            flops=flops, bytes_accessed=12 * 2**20, transcendentals=ROWS * PADDED
        ),
    )


def exchange(copies, axes):
    return lax.all_to_all(copies, axes, 0, 0, tiled=True)


def swap(rows):
    return lax.ppermute(rows, "core", [(i, i ^ 1) for i in range(lax.axis_size("core"))])


def pair_sum(rows):
    plane = lax.axis_size(PLANE)
    near = lax.axis_index("core") == 0
    halves = rows.reshape(2, plane, -1, LANES)
    mine = jnp.where(near, halves[0], halves[1])
    return mine + swap(jnp.where(near, halves[1], halves[0]))


def plane_sum(mine):
    return jnp.sum(exchange(mine, PLANE), axis=0)


def all_parts(mine):
    plane, line = lax.axis_size(PLANE), lax.axis_size("x")
    near = lax.axis_index("core") == 0
    mine = jnp.sum(exchange(jnp.broadcast_to(mine[None], (line,) + mine.shape), "x"), axis=0)
    half = exchange(jnp.broadcast_to(mine[None], (plane,) + mine.shape), PLANE)
    other = swap(half)
    return jnp.stack([jnp.where(near, half, other), jnp.where(near, other, half)])


def tie(first, second):
    return lax.optimization_barrier((first, second))


def per_device(
    block_input,
    cotangent,
    w_expand,
    gain_expand,
    shift_expand,
    w_depth,
    gain_depth,
    shift_depth,
    w_reduce,
    b_reduce,
    w_restore,
    b_restore,
    w_project,
    gain_project,
    upper_grads,
):
    peers = lax.axis_size(GROUP)
    images_total = lax.axis_size(AXES)
    extra = PADDED - HID
    images, cot = block_input[0, 0], cotangent[0, 0]
    wexp = jnp.pad(w_expand, ((0, 0), (0, extra)))
    wproj = jnp.pad(w_project, ((0, extra), (0, 0)))
    wproj_turn = jnp.pad(w_project.T, ((0, 0), (0, extra)))
    wexp_turn = jnp.pad(w_expand.T, ((0, extra), (0, 0)))
    wred = jnp.pad(w_reduce.astype(F32).T, ((0, SE_ROWS - SE), (0, extra)))
    wres = jnp.pad(w_restore.astype(F32), ((0, SE_ROWS - SE), (0, extra)))
    bred = jnp.broadcast_to(jnp.pad(b_reduce, (0, SE_ROWS - SE))[:, None], (SE_ROWS, LANES))
    bres = jnp.pad(b_restore, (0, extra))[None]
    table = jnp.concatenate(
        [w_depth.astype(F32)]
        + [v[None] for v in (gain_expand, shift_expand, gain_depth, shift_depth)],
        axis=0,
    )
    table = jnp.pad(table, ((0, TABLE - table.shape[0]), (0, extra)))
    xpad_spec, w_spec = whole((ROWS, C)), lane_block(C)
    se_spec = whole((SE_ROWS, PADDED))
    stat_out = (peer_block(peers), f32(peers, 2, PADDED))
    stat_whole = (whole((peers, 2, PADDED)), f32(peers, 2, PADDED))
    moments = (lane_block(8), f32(8, PADDED))
    map_f32 = pltpu.VMEM((ROWS, LANES), F32)
    map_bf16 = pltpu.VMEM((ROWS, LANES), BF16)
    line = pltpu.VMEM((2, WIDE, C), F32)
    taps = pltpu.VMEM((KER * KER * 8, LANES), F32)
    halo = pltpu.VMEM((HALO, LANES), F32)
    matmul = 2 * ROWS * C * PADDED

    xpad, stat = call(
        stats_kernel,
        [whole((SIDE, SIDE, C)), w_spec],
        [(xpad_spec, EDGE_BF16), stat_out],
        [map_f32, line],
        matmul,
    )(images, wexp)
    gathered = exchange(stat, GROUP)
    depth, stat, moment_one = call(
        forward_kernel,
        [xpad_spec, w_spec, peer_block(peers), lane_block(TABLE)],
        [(MAP_BLOCK, MAP), stat_out, moments],
        [map_f32, halo, taps],
        50 * ROWS * PADDED,
    )(xpad, wexp, gathered, table)
    gathered = exchange(stat, GROUP)
    moment_two, project, cpad, vector, column, stat = call(
        project_kernel,
        [
            MAP_BLOCK,
            peer_block(peers),
            lane_block(TABLE),
            whole((PADDED, C)),
            whole((SIDE, SIDE, C)),
            se_spec,
            se_spec,
            whole((SE_ROWS, LANES)),
            whole((1, PADDED)),
        ],
        [
            moments,
            (whole((ROWS, C)), EDGE),
            (whole((ROWS, C)), EDGE_BF16),
            (whole((8, PADDED)), f32(8, PADDED)),
            (whole((2, SE_ROWS, LANES)), f32(2, SE_ROWS, LANES)),
            (whole((peers, 4, C)), f32(peers, 4, C)),
        ],
        [
            pltpu.VMEM((CHUNKS, ROWS, LANES), BF16),
            pltpu.VMEM((ROWS, PADDED), BF16),
            line,
        ],
        matmul,
    )(depth, gathered, table, wproj, cot, wred, wres, bred, bres)
    gathered = exchange(stat, GROUP)
    first, slope, hidden, gpp, rows, reduce, stat = call(
        back_project_kernel,
        [
            MAP_BLOCK,
            whole((peers, 4, C)),
            lane_block(TABLE),
            lane_block(8),
            whole((ROWS, C)),
            whole((ROWS, C)),
            whole((1, C)),
            w_spec,
            whole((8, PADDED)),
            whole((2, SE_ROWS, LANES)),
            se_spec,
            se_spec,
        ],
        [
            (MAP_BLOCK, MAP),
            (MAP_BLOCK, MAP),
            (MAP_BLOCK, MAP_BF16),
            (whole((ROWS, C)), EDGE_BF16),
            (whole((8, PADDED)), f32(8, PADDED)),
            (whole((SE_ROWS, LANES)), f32(SE_ROWS, LANES)),
            stat_whole,
        ],
        [map_f32, pltpu.VMEM((8, PADDED), F32)],
        2 * matmul,
    )(
        depth,
        gathered,
        table,
        moment_two,
        project,
        cpad,
        gain_project[None],
        wproj_turn,
        vector,
        column,
        wred,
        wres,
    )
    gathered = exchange(stat, GROUP)
    (early,) = call(
        early_kernel,
        [
            whole((ROWS, C)),
            MAP_BLOCK,
            lane_block(8),
            whole((SE_ROWS, LANES)),
            lane_block(8),
            whole((2, SE_ROWS, LANES)),
            whole((UPPER_ROWS, LANES)),
        ],
        [(whole((EARLY_ROWS, LANES)), f32(EARLY_ROWS, LANES))],
        [],
        10 * matmul,
    )(gpp, hidden, rows, reduce, vector, column, upper_grads[0].reshape(-1, LANES))
    early, gathered = tie(pair_sum(early), gathered)
    early = plane_sum(early)
    grad_one, stat, sums, field, back = call(
        back_depth_kernel,
        [
            MAP_BLOCK,
            MAP_BLOCK,
            MAP_BLOCK,
            peer_block(peers),
            lane_block(TABLE),
            lane_block(8),
            lane_block(8),
            lane_block(8),
            lane_block(8),
            xpad_spec,
            w_spec,
        ],
        [
            (MAP_BLOCK, MAP),
            stat_out,
            (lane_block(8), f32(8, PADDED)),
            (MAP_BLOCK, MAP_BF16),
            (MAP_BLOCK, MAP),
        ],
        [map_f32, halo, map_f32, taps],
        100 * ROWS * PADDED,
    )(depth, first, slope, gathered, table, moment_two, moment_one, vector, rows, xpad, wexp)
    stat, early, field = lax.optimization_barrier((stat, early, field))
    gathered = exchange(stat, GROUP)
    (sums,) = call(
        kernel_grad_kernel,
        [MAP_BLOCK, MAP_BLOCK, lane_block(8)],
        [(lane_block(TABLE), f32(TABLE, PADDED))],
        [halo],
        50 * ROWS * PADDED,
    )(field, back, sums)
    input_grad, late = call(
        back_expand_kernel,
        [
            MAP_BLOCK,
            peer_block(peers),
            lane_block(TABLE),
            lane_block(8),
            xpad_spec,
            w_spec,
            lane_block(TABLE),
            xpad_spec,
            whole((C, ROWS)),
            whole((PADDED, C)),
        ],
        [
            (whole((SIDE, SIDE, C)), jax.ShapeDtypeStruct((SIDE, SIDE, C), BF16)),
            (whole((LATE_ROWS, LANES)), f32(LATE_ROWS, LANES)),
        ],
        [map_f32, pltpu.VMEM((ROWS, PADDED), BF16), pltpu.VMEM((ROWS, C), F32)],
        3 * matmul,
    )(grad_one, gathered, table, moment_one, xpad, wexp, sums, cpad, xpad.T, wexp_turn)

    late = plane_sum(pair_sum(late))
    split = early.shape[0]
    full = all_parts(jnp.concatenate([early, late]))
    early = full[:, :, :split].reshape(EARLY_ROWS, LANES)
    late = full[:, :, split:].reshape(LATE_ROWS, LANES)

    scale = 1.0 / images_total
    wide = (1, HID)
    g_project, g_restore, g_reduce, g_brestore, g_shift_two, g_gain_two, g_gproject, g_breduce, upper = (
        unpack(
            unpack_early_kernel,
            early,
            [(C, HID), (SE, HID), (SE, HID), wide, wide, wide, (1, C), (1, SE), (UPPER_ROWS, LANES)],
            scale,
        )
    )
    g_expand, g_depth, g_shift_one, g_gain_one = unpack(
        unpack_late_kernel, late, [(C, HID), (KER * KER, HID), wide, wide], scale
    )
    return (
        input_grad[None, None],
        g_expand,
        g_gain_one[0],
        g_shift_one[0],
        g_depth,
        g_gain_two[0],
        g_shift_two[0],
        g_reduce.T,
        g_breduce[0],
        g_restore,
        g_brestore[0],
        g_project.T,
        g_gproject[0],
        upper.reshape(-1),
    )


def solution(mesh):
    chips = Mesh(mesh.devices.reshape(SHAPE), AXES)
    maps = P(("z", "core"), GROUP, None, None, None)
    return jax.shard_map(
        per_device,
        mesh=chips,
        in_specs=(maps, maps) + (P(),) * 12 + (P(AXES, None),),
        out_specs=(maps,) + (P(),) * 13,
        check_vma=False,
    )
```

```python
import functools

import jax
import jax.numpy as jnp
from jax import lax
from jax.experimental import pallas as pl
from jax.experimental.pallas import tpu as pltpu
from jax.sharding import Mesh, PartitionSpec as P

KER = 5
EPSILON = 0.001
SHAPE = (4, 8, 8, 2)
AXES = ("x", "y", "z", "core")
GROUP = ("x", "y")
PLANE = ("y", "z")
SIDE = 29
WIDE = 32
ROWS = SIDE * WIDE
HALO = (SIDE + KER - 1) * WIDE
C = 176
HID = 1056
LANES = 128
CHUNKS = 9
PADDED = CHUNKS * LANES
SE = 44
SE_ROWS = 48
SPOTS = SIDE * SIDE
GAIN_ONE, SHIFT_ONE, GAIN_TWO, SHIFT_TWO, BIAS = 25, 26, 27, 28, 29
TABLE = 32
EARLY = C + 2 * SE_ROWS
UPPER_AT = CHUNKS * EARLY
UPPER_ROWS = 1024
EARLY_ROWS = 3584
LATE = C + TABLE
LATE_ROWS = 2048
PIECE = 4
RESIDENT = 20 * 2**20
STREAMED = 56 * 2**20
F32 = jnp.float32
BF16 = jnp.bfloat16


def dot(left, right, left_dim=1, right_dim=0):
    return lax.dot_general(
        left, right, (((left_dim,), (right_dim,)), ((), ())), preferred_element_type=F32
    )


def logistic(values):
    return 0.5 + 0.5 * jnp.tanh(0.5 * values)


def valid_mask(lanes=LANES):
    return lax.broadcasted_iota(jnp.int32, (WIDE, lanes), 0) < SIDE


def row_at(index):
    if isinstance(index, int):
        return slice(index * WIDE, (index + 1) * WIDE)
    return pl.ds(pl.multiple_of(index * WIDE, WIDE), WIDE)


def each_row(body, init):
    for i in range(SIDE):
        init = body(i, init)
    return init


def loop_rows(body, init):
    return lax.fori_loop(0, SIDE, body, init)


def col_sum(values):
    return jnp.sum(values, axis=0, keepdims=True)


def zeros(lanes=LANES):
    return jnp.zeros((WIDE, lanes), F32)


def share(pair, ref):
    ref[...] = jnp.broadcast_to(pair[None], ref.shape)


def pair_rows(first, second):
    return jnp.where(lax.broadcasted_iota(jnp.int32, (2, first.shape[1]), 0) == 0, first, second)


def spread_of(ref, mean, mask):
    def body(i, acc):
        dev = jnp.where(mask, ref[row_at(i), :] - mean, 0.0)
        return acc + dev * dev

    return col_sum(each_row(body, zeros(mean.shape[1]))) / SPOTS


def merged(gathered):
    peers = gathered.shape[0]
    total = jnp.sum(gathered, axis=0)
    center = total[0:1] / peers
    dev = jnp.sum(jnp.square(gathered[:, 0:1, :] - center[None]), axis=0)
    spread = (total[1:2] + dev) / peers
    return center, lax.rsqrt(spread + EPSILON)


def widen(map_ref, flat_ref, line_ref):
    line_ref[...] = jnp.zeros_like(line_ref)
    for i in range(SIDE):
        line_ref[i % 2, 0:SIDE, :] = map_ref[i].astype(F32)
        flat_ref[i * WIDE : (i + 1) * WIDE, :] = line_ref[i % 2].astype(BF16)


def stats_kernel(x_ref, w_ref, xpad_ref, stat_ref, pre_ref, line_ref):
    @pl.when(pl.program_id(0) == 0)
    def _():
        widen(x_ref, xpad_ref, line_ref)

    pre_ref[...] = dot(xpad_ref[...], w_ref[...])
    total = each_row(lambda i, acc: acc + pre_ref[row_at(i), :], zeros())
    mean = col_sum(total) / SPOTS
    share(pair_rows(mean, spread_of(pre_ref, mean, valid_mask())), stat_ref)


def slide(parts, sign):
    out = parts[2]
    for b in (0, 1, 3, 4):
        out = out + pltpu.roll(parts[b], (sign * (2 - b)) % WIDE, 0)
    return out


def row_taps(halo_ref, tap_ref, i, flip):
    parts = [None] * KER
    for a in range(KER):
        source = halo_ref[row_at(i + a), :].reshape(WIDE // 8, 8, LANES)
        for b in range(KER):
            k = ((KER - 1 - a) if flip else a) * KER + b
            term = source * tap_ref[k * 8 : k * 8 + 8, :]
            parts[b] = term if parts[b] is None else parts[b] + term
    return slide([part.reshape(WIDE, LANES) for part in parts], -1 if flip else 1)


def clear_halo(ref):
    edge = jnp.zeros((2 * WIDE, LANES), F32)
    ref[0 : 2 * WIDE, :] = edge
    ref[HALO - 2 * WIDE : HALO, :] = edge


def spread_taps(table_ref, tap_ref):
    for k in range(KER * KER):
        tap_ref[k * 8 : k * 8 + 8, :] = jnp.broadcast_to(table_ref[k : k + 1, :], (8, LANES))


def forward_kernel(
    xpad_ref,
    w_ref,
    gathered_ref,
    table_ref,
    depth_ref,
    stat_ref,
    moment_ref,
    pre_ref,
    halo_ref,
    tap_ref,
):
    @pl.when(pl.program_id(0) == 0)
    def _():
        clear_halo(halo_ref)

    mask = valid_mask()
    center, scale = merged(gathered_ref[...])
    moment_ref[0:1, :] = center
    moment_ref[1:2, :] = scale
    slope = scale * table_ref[GAIN_ONE : GAIN_ONE + 1, :]
    offset = table_ref[SHIFT_ONE : SHIFT_ONE + 1, :] - center * slope
    pre_ref[...] = dot(xpad_ref[...], w_ref[...])

    def activate(i, _):
        act = pre_ref[row_at(i), :] * slope + offset
        silu = (act * logistic(act)).astype(BF16).astype(F32)
        halo_ref[row_at(i + 2), :] = jnp.where(mask, silu, 0.0)
        return 0

    each_row(activate, 0)
    spread_taps(table_ref, tap_ref)

    def filter_row(i, acc):
        out = jnp.where(mask, row_taps(halo_ref, tap_ref, i, False), 0.0)
        depth_ref[row_at(i), :] = out
        return acc + out

    mean = col_sum(loop_rows(filter_row, zeros())) / SPOTS
    share(pair_rows(mean, spread_of(depth_ref, mean, mask)), stat_ref)


def lanes_at(index):
    return pl.ds(pl.multiple_of(index * LANES, LANES), LANES)


def project_kernel(
    depth_ref,
    gathered_ref,
    table_ref,
    wproject_ref,
    cot_ref,
    wreduce_ref,
    wrestore_ref,
    breduce_ref,
    brestore_ref,
    moment_ref,
    project_ref,
    cpad_ref,
    vector_ref,
    column_ref,
    stat_ref,
    act_ref,
    hidden_ref,
    line_ref,
):
    step = pl.program_id(0)
    mask = valid_mask()
    center, scale = merged(gathered_ref[...])
    moment_ref[0:1, :] = center
    moment_ref[1:2, :] = scale
    slope = scale * table_ref[GAIN_TWO : GAIN_TWO + 1, :]
    offset = table_ref[SHIFT_TWO : SHIFT_TWO + 1, :] - center * slope

    def activate(i, acc):
        act = depth_ref[row_at(i), :] * slope + offset
        silu = jnp.where(mask, act * logistic(act), 0.0).astype(BF16)
        act_ref[step, row_at(i), :] = silu
        return acc + silu.astype(F32)

    vector_ref[0:1, lanes_at(step)] = col_sum(each_row(activate, zeros())) / SPOTS

    @pl.when(step == 0)
    def _():
        widen(cot_ref, cpad_ref, line_ref)

    @pl.when(step == CHUNKS - 1)
    def _():
        pooled = vector_ref[0:1, :]
        logit = jnp.sum(wreduce_ref[...] * pooled, axis=1, keepdims=True) + breduce_ref[...]
        squeezed = logit * logistic(logit)
        column_ref[0] = logit
        column_ref[1] = squeezed
        restored = col_sum(wrestore_ref[...] * squeezed[:, 0:1]) + brestore_ref[...]
        vector_ref[1:2, :] = logistic(restored)

        def fill(c, _):
            excite = vector_ref[1:2, lanes_at(c)]

            def scale_row(i, _):
                hidden_ref[row_at(i), lanes_at(c)] = (
                    act_ref[c, row_at(i), :].astype(F32) * excite
                ).astype(BF16)
                return 0

            each_row(scale_row, 0)
            return 0

        lax.fori_loop(0, CHUNKS, fill, 0)
        project_ref[...] = dot(hidden_ref[...], wproject_ref[...])

        def sums(i, accs):
            values, incoming = project_ref[row_at(i), :], cpad_ref[row_at(i), :].astype(F32)
            return accs[0] + values, accs[1] + incoming

        total, cot_total = each_row(sums, (zeros(C), zeros(C)))
        mean = col_sum(total) / SPOTS

        def devs(i, accs):
            dev = jnp.where(valid_mask(C), project_ref[row_at(i), :] - mean, 0.0)
            incoming = cpad_ref[row_at(i), :].astype(F32)
            return accs[0] + dev * dev, accs[1] + incoming * dev

        square, cross = each_row(devs, (zeros(C), zeros(C)))
        row = lax.broadcasted_iota(jnp.int32, (4, C), 0)
        packed = jnp.where(
            row == 0,
            mean,
            jnp.where(
                row == 1,
                col_sum(square) / SPOTS,
                jnp.where(row == 2, col_sum(cot_total), col_sum(cross)),
            ),
        )
        share(packed, stat_ref)


def back_project_kernel(
    depth_ref,
    gathered_ref,
    table_ref,
    moment_ref,
    project_ref,
    cpad_ref,
    gain_ref,
    wproject_ref,
    vector_ref,
    column_ref,
    wreduce_ref,
    wrestore_ref,
    hidden_ref,
    gpp_ref,
    row_ref,
    reduce_ref,
    stat_ref,
    back_ref,
    sums_ref,
):
    step = pl.program_id(0)
    mask = valid_mask()

    @pl.when(step == 0)
    def _():
        gathered = gathered_ref[...]
        peers = gathered.shape[0]
        count = peers * SPOTS
        total = jnp.sum(gathered, axis=0)
        center3 = total[0:1] / peers
        away = gathered[:, 0:1, :] - center3[None]
        spread = (total[1:2] + jnp.sum(jnp.square(away), axis=0)) / peers
        scale3 = lax.rsqrt(spread + EPSILON)
        cross = total[3:4] + jnp.sum(gathered[:, 2:3, :] * away, axis=0)
        first = total[2:3] / count
        second = cross * scale3 / count
        factor = scale3 * gain_ref[...]
        wide = valid_mask(C)

        def body(i, acc):
            normed = (project_ref[row_at(i), :] - center3) * scale3
            incoming = cpad_ref[row_at(i), :].astype(F32)
            grad = factor * (incoming - first - normed * second)
            gpp_ref[row_at(i), :] = jnp.where(wide, grad, 0.0).astype(BF16)
            return acc + incoming * normed

        row_ref[...] = jnp.zeros_like(row_ref)
        row_ref[4:5, 0:C] = col_sum(each_row(body, zeros(C)))

    center, scale = moment_ref[0:1, :], moment_ref[1:2, :]
    gain = table_ref[GAIN_TWO : GAIN_TWO + 1, :]
    shift = table_ref[SHIFT_TWO : SHIFT_TWO + 1, :]
    excite = vector_ref[1:2, lanes_at(step)]
    back_ref[...] = dot(gpp_ref[...], wproject_ref[...])

    def body(i, accs):
        normed = (depth_ref[row_at(i), :] - center) * scale
        act = normed * gain + shift
        sig = logistic(act)
        silu = (act * sig).astype(BF16).astype(F32)
        slope = jnp.where(mask, sig * (1.0 + act * (1.0 - sig)), 0.0)
        hidden_ref[row_at(i), :] = jnp.where(mask, silu * excite, 0.0).astype(BF16)
        back = back_ref[row_at(i), :]
        first = back * slope
        return (
            accs[0] + back * silu,
            accs[1] + first,
            accs[2] + first * normed,
            accs[3] + slope,
            accs[4] + slope * normed,
        )

    totals = each_row(body, tuple(zeros() for _ in range(5)))
    for k in range(5):
        sums_ref[k : k + 1, lanes_at(step)] = col_sum(totals[k])

    @pl.when(step == CHUNKS - 1)
    def _():
        excite = vector_ref[1:2, :]
        logit = column_ref[0]
        grad_logit = sums_ref[0:1, :] * excite * (1.0 - excite)
        grad_squeezed = jnp.sum(wrestore_ref[...] * grad_logit, axis=1, keepdims=True)
        sig = logistic(logit)
        grad_reduce = grad_squeezed * (sig * (1.0 + logit * (1.0 - sig)))
        grad_pooled = col_sum(wreduce_ref[...] * grad_reduce[:, 0:1]) / SPOTS
        shift_sum = excite * sums_ref[1:2, :] + grad_pooled * sums_ref[3:4, :]
        gain_sum = excite * sums_ref[2:3, :] + grad_pooled * sums_ref[4:5, :]
        share(pair_rows(shift_sum, gain_sum), stat_ref)
        row_ref[0:1, :] = grad_pooled
        row_ref[1:2, :] = grad_logit
        row_ref[2:3, :] = shift_sum
        row_ref[3:4, :] = gain_sum
        reduce_ref[...] = grad_reduce


def early_kernel(
    gpp_ref, hidden_ref, row_ref, reduce_ref, vector_ref, column_ref, upper_ref, grads_ref
):
    step = pl.program_id(0)
    base = pl.multiple_of(step * EARLY, 16)
    grads_ref[pl.ds(base, C), :] = dot(gpp_ref[...], hidden_ref[...], 0, 0)
    lane = lax.broadcasted_iota(jnp.int32, (SE_ROWS, LANES), 1)
    row = lax.broadcasted_iota(jnp.int32, (SE_ROWS, LANES), 0)
    squeezed, grad_reduce = column_ref[1], reduce_ref[...]
    block = squeezed * row_ref[1:2, :]
    block = jnp.where(row == SE, row_ref[1:2, :], block)
    block = jnp.where(row == SE + 1, row_ref[2:3, :], block)
    block = jnp.where(row == SE + 2, row_ref[3:4, :], block)
    bias_row = col_sum(jnp.where(lane == row, grad_reduce, 0.0))
    extra = jnp.where(step < 2, row_ref[4:5, :], bias_row)
    block = jnp.where(row == SE + 3, extra, block)
    grads_ref[pl.ds(pl.multiple_of(base + C, 16), SE_ROWS), :] = block
    grads_ref[pl.ds(pl.multiple_of(base + C + SE_ROWS, 16), SE_ROWS), :] = (
        grad_reduce * vector_ref[0:1, :]
    )

    @pl.when(step == 0)
    def _():
        grads_ref[UPPER_AT : UPPER_AT + UPPER_ROWS, :] = upper_ref[...]
        rest = EARLY_ROWS - UPPER_AT - UPPER_ROWS
        grads_ref[UPPER_AT + UPPER_ROWS :, :] = jnp.zeros((rest, LANES), F32)


def back_depth_kernel(
    depth_ref,
    gpp_ref,
    wproject_ref,
    gathered_ref,
    table_ref,
    moment_two_ref,
    moment_one_ref,
    vector_ref,
    pooled_ref,
    xpad_ref,
    w_ref,
    grad_ref,
    stat_ref,
    sums_ref,
    field_ref,
    back_ref,
    pre_ref,
    ghalo_ref,
    side_ref,
    tap_ref,
    product_ref,
):
    @pl.when(pl.program_id(0) == 0)
    def _():
        clear_halo(ghalo_ref)

    mask = valid_mask()
    total = jnp.sum(gathered_ref[...], axis=0)
    gain = table_ref[GAIN_TWO : GAIN_TWO + 1, :]
    count = gathered_ref.shape[0] * SPOTS
    mean_first = gain * total[0:1] / count
    mean_second = gain * total[1:2] / count
    center, scale = moment_two_ref[0:1, :], moment_two_ref[1:2, :]
    shift = table_ref[SHIFT_TWO : SHIFT_TWO + 1, :]
    excite = vector_ref[1:2, :] * gain
    pooled = pooled_ref[0:1, :] * gain
    product_ref[...] = dot(gpp_ref[...], wproject_ref[...])
    center_one, scale_one = moment_one_ref[0:1, :], moment_one_ref[1:2, :]
    slope_one = scale_one * table_ref[GAIN_ONE : GAIN_ONE + 1, :]
    offset_one = table_ref[SHIFT_ONE : SHIFT_ONE + 1, :] - center_one * slope_one
    pre_ref[...] = dot(xpad_ref[...], w_ref[...])

    def prepare(i, _):
        normed = (depth_ref[row_at(i), :] - center) * scale
        act = normed * gain + shift
        sig = logistic(act)
        grad = (product_ref[row_at(i), :] * excite + pooled) * (sig * (1.0 + act * (1.0 - sig)))
        grad = jnp.where(mask, scale * (grad - mean_first - normed * mean_second), 0.0)
        ghalo_ref[row_at(i + 2), :] = grad
        back_ref[row_at(i), :] = grad.astype(BF16)
        act = pre_ref[row_at(i), :] * slope_one + offset_one
        sig = logistic(act)
        field_ref[row_at(i), :] = jnp.where(mask, act * sig, 0.0).astype(BF16)
        side_ref[row_at(i), :] = jnp.where(mask, sig * (1.0 + act * (1.0 - sig)), 0.0)
        return 0

    each_row(prepare, 0)
    spread_taps(table_ref, tap_ref)

    def input_grad(i, accs):
        grad = row_taps(ghalo_ref, tap_ref, i, True) * side_ref[row_at(i), :]
        grad_ref[row_at(i), :] = grad
        normed = (pre_ref[row_at(i), :] - center_one) * scale_one
        return accs[0] + grad, accs[1] + grad * normed

    shift_sum, gain_sum = (col_sum(a) for a in loop_rows(input_grad, (zeros(), zeros())))
    share(pair_rows(shift_sum, gain_sum), stat_ref)
    sums_ref[...] = jnp.zeros_like(sums_ref)
    sums_ref[0:1, :] = shift_sum
    sums_ref[1:2, :] = gain_sum


def kernel_grad_kernel(field_ref, back_ref, sums_ref, out_ref, halo_ref):
    @pl.when(pl.program_id(0) == 0)
    def _():
        clear_halo(halo_ref)

    halo_ref[2 * WIDE : 2 * WIDE + ROWS, :] = field_ref[...].astype(F32)

    def kernel_grad(i, accs):
        grad = back_ref[row_at(i), :].astype(F32)
        shifted = [
            (grad if b == 2 else pltpu.roll(grad, (b - 2) % WIDE, 0)).reshape(
                WIDE // 8, 8, LANES
            )
            for b in range(KER)
        ]
        accs = list(accs)
        for a in range(KER):
            field = halo_ref[row_at(i + a), :].reshape(WIDE // 8, 8, LANES)
            for b in range(KER):
                accs[a * KER + b] = accs[a * KER + b] + jnp.sum(field * shifted[b], axis=0)
        return tuple(accs)

    start = tuple(jnp.zeros((8, LANES), F32) for _ in range(KER * KER))
    accs = loop_rows(kernel_grad, start)
    for k in range(KER * KER):
        out_ref[k : k + 1, :] = col_sum(accs[k])
    out_ref[25:TABLE, :] = sums_ref[0 : TABLE - 25, :]


def back_expand_kernel(
    grad_ref,
    gathered_ref,
    table_ref,
    moment_ref,
    xpad_ref,
    w_ref,
    sums_ref,
    cpad_ref,
    xturn_ref,
    wturn_ref,
    out_ref,
    grads_ref,
    pre_ref,
    gpe_ref,
    acc_ref,
):
    step = pl.program_id(0)
    mask = valid_mask()
    total = jnp.sum(gathered_ref[...], axis=0)
    count = gathered_ref.shape[0] * SPOTS
    mean_first, mean_second = total[0:1] / count, total[1:2] / count
    center, scale = moment_ref[0:1, :], moment_ref[1:2, :]
    factor = scale * table_ref[GAIN_ONE : GAIN_ONE + 1, :]
    pre_ref[...] = dot(xpad_ref[...], w_ref[...])

    def body(i, _):
        normed = (pre_ref[row_at(i), :] - center) * scale
        grad = factor * (grad_ref[row_at(i), :] - mean_first - normed * mean_second)
        gpe_ref[row_at(i), lanes_at(step)] = jnp.where(mask, grad, 0.0).astype(BF16)
        return 0

    each_row(body, 0)
    base = pl.multiple_of(step * LATE, 16)
    grads_ref[pl.ds(base, C), :] = dot(xturn_ref[...], gpe_ref[:, lanes_at(step)])
    grads_ref[pl.ds(pl.multiple_of(base + C, 16), TABLE), :] = sums_ref[...]

    @pl.when(step == CHUNKS - 1)
    def _():
        grads_ref[CHUNKS * LATE :, :] = jnp.zeros((LATE_ROWS - CHUNKS * LATE, LANES), F32)
        acc_ref[...] = cpad_ref[...].astype(F32) + dot(gpe_ref[...], wturn_ref[...])
        for i in range(SIDE):
            out_ref[i] = acc_ref[i * WIDE : i * WIDE + SIDE, :].astype(BF16)


def put_row(ref, rows_ref, row, height, scale):
    for c in range(-(-ref.shape[-1] // LANES)):
        width = min(LANES, ref.shape[-1] - c * LANES)
        at = c * height + row
        if len(ref.shape) == 1:
            ref[c * LANES : c * LANES + width] = rows_ref[at, 0:width] * scale
            continue
        ref[:, c * LANES : c * LANES + width] = rows_ref[at : at + ref.shape[0], 0:width] * scale


def unpack_early_kernel(
    scale,
    rows_ref,
    project_ref,
    restore_ref,
    reduce_ref,
    brestore_ref,
    shift_ref,
    gain_ref,
    gproject_ref,
    breduce_ref,
    upper_ref,
):
    put_row(project_ref, rows_ref, 0, EARLY, scale)
    put_row(restore_ref, rows_ref, C, EARLY, scale)
    put_row(reduce_ref, rows_ref, C + SE_ROWS, EARLY, scale)
    put_row(brestore_ref, rows_ref, C + SE, EARLY, scale)
    put_row(shift_ref, rows_ref, C + SE + 1, EARLY, scale)
    put_row(gain_ref, rows_ref, C + SE + 2, EARLY, scale)
    put_row(gproject_ref, rows_ref, C + SE + 3, EARLY, scale)
    at = 2 * EARLY + C + SE + 3
    breduce_ref[...] = rows_ref[at, 0:SE] * scale
    upper_ref[...] = rows_ref[UPPER_AT : UPPER_AT + UPPER_ROWS, :]


def unpack_late_kernel(scale, rows_ref, expand_ref, depth_ref, shift_ref, gain_ref):
    put_row(expand_ref, rows_ref, 0, LATE, scale)
    put_row(depth_ref, rows_ref, C, LATE, scale)
    put_row(shift_ref, rows_ref, C + 25, LATE, scale)
    put_row(gain_ref, rows_ref, C + 26, LATE, scale)


def unpack(kernel, rows, shapes, scale):
    return pl.pallas_call(
        functools.partial(kernel, scale),
        out_shape=tuple(f32(*shape) for shape in shapes),
        compiler_params=pltpu.CompilerParams(vmem_limit_bytes=RESIDENT),
        cost_estimate=pl.CostEstimate(
            flops=rows.size, bytes_accessed=8 * rows.size, transcendentals=0
        ),
    )(rows)


def whole(shape):
    return pl.BlockSpec(shape, lambda c: (0,) * len(shape))


def lane_block(rows):
    return pl.BlockSpec((rows, LANES), lambda c: (0, c))


def peer_block(peers):
    return pl.BlockSpec((peers, 2, LANES), lambda c: (0, 0, c))


MAP_BLOCK = pl.BlockSpec((pl.squeezed, ROWS, LANES), lambda c: (c, 0, 0))
MAP = jax.ShapeDtypeStruct((CHUNKS, ROWS, LANES), F32)
MAP_BF16 = jax.ShapeDtypeStruct((CHUNKS, ROWS, LANES), BF16)
EDGE = jax.ShapeDtypeStruct((ROWS, C), F32)
EDGE_BF16 = jax.ShapeDtypeStruct((ROWS, C), BF16)


def f32(*shape):
    return jax.ShapeDtypeStruct(shape, F32)


def call(kernel, ins, outs, scratch, flops, vmem=RESIDENT):
    return pl.pallas_call(
        kernel,
        grid=(CHUNKS,),
        in_specs=ins,
        out_specs=tuple(spec for spec, _ in outs),
        out_shape=tuple(shape for _, shape in outs),
        scratch_shapes=scratch,
        compiler_params=pltpu.CompilerParams(vmem_limit_bytes=vmem),
        cost_estimate=pl.CostEstimate(
            flops=flops, bytes_accessed=12 * 2**20, transcendentals=ROWS * PADDED
        ),
    )


def exchange(copies, axes):
    return lax.all_to_all(copies, axes, 0, 0, tiled=True)


def swap(rows):
    return lax.ppermute(rows, "core", [(i, i ^ 1) for i in range(lax.axis_size("core"))])


def pair_sum(rows):
    plane = lax.axis_size(PLANE)
    near = lax.axis_index("core") == 0
    halves = rows.reshape(2, plane, -1, PIECE, LANES)
    mine = jnp.where(near, halves[0], halves[1])
    return mine + swap(jnp.where(near, halves[1], halves[0]))


def plane_sum(mine):
    return jnp.sum(exchange(mine, PLANE), axis=0)


def all_parts(mine):
    plane, line = lax.axis_size(PLANE), lax.axis_size("x")
    near = lax.axis_index("core") == 0
    mine = jnp.sum(exchange(jnp.broadcast_to(mine[None], (line,) + mine.shape), "x"), axis=0)
    half = exchange(jnp.broadcast_to(mine[None], (plane,) + mine.shape), PLANE)
    other = swap(half)
    return jnp.stack([jnp.where(near, half, other), jnp.where(near, other, half)])


def tie(first, second):
    return lax.optimization_barrier((first, second))


def per_device(
    block_input,
    cotangent,
    w_expand,
    gain_expand,
    shift_expand,
    w_depth,
    gain_depth,
    shift_depth,
    w_reduce,
    b_reduce,
    w_restore,
    b_restore,
    w_project,
    gain_project,
    upper_grads,
):
    peers = lax.axis_size(GROUP)
    images_total = lax.axis_size(AXES)
    extra = PADDED - HID
    images, cot = block_input[0, 0], cotangent[0, 0]
    wexp = jnp.pad(w_expand, ((0, 0), (0, extra)))
    wproj = jnp.pad(w_project, ((0, extra), (0, 0)))
    wproj_turn = jnp.pad(w_project.T, ((0, 0), (0, extra)))
    wexp_turn = jnp.pad(w_expand.T, ((0, extra), (0, 0)))
    wred = jnp.pad(w_reduce.astype(F32).T, ((0, SE_ROWS - SE), (0, extra)))
    wres = jnp.pad(w_restore.astype(F32), ((0, SE_ROWS - SE), (0, extra)))
    bred = jnp.broadcast_to(jnp.pad(b_reduce, (0, SE_ROWS - SE))[:, None], (SE_ROWS, LANES))
    bres = jnp.pad(b_restore, (0, extra))[None]
    table = jnp.concatenate(
        [w_depth.astype(F32)]
        + [v[None] for v in (gain_expand, shift_expand, gain_depth, shift_depth)],
        axis=0,
    )
    table = jnp.pad(table, ((0, TABLE - table.shape[0]), (0, extra)))
    xpad_spec, w_spec = whole((ROWS, C)), lane_block(C)
    se_spec = whole((SE_ROWS, PADDED))
    stat_out = (peer_block(peers), f32(peers, 2, PADDED))
    stat_whole = (whole((peers, 2, PADDED)), f32(peers, 2, PADDED))
    moments = (lane_block(8), f32(8, PADDED))
    map_f32 = pltpu.VMEM((ROWS, LANES), F32)
    map_bf16 = pltpu.VMEM((ROWS, LANES), BF16)
    line = pltpu.VMEM((2, WIDE, C), F32)
    taps = pltpu.VMEM((KER * KER * 8, LANES), F32)
    halo = pltpu.VMEM((HALO, LANES), F32)
    matmul = 2 * ROWS * C * PADDED

    xpad, stat = call(
        stats_kernel,
        [whole((SIDE, SIDE, C)), w_spec],
        [(xpad_spec, EDGE_BF16), stat_out],
        [map_f32, line],
        matmul,
    )(images, wexp)
    gathered = exchange(stat, GROUP)
    depth, stat, moment_one = call(
        forward_kernel,
        [xpad_spec, w_spec, peer_block(peers), lane_block(TABLE)],
        [(MAP_BLOCK, MAP), stat_out, moments],
        [map_f32, halo, taps],
        50 * ROWS * PADDED,
    )(xpad, wexp, gathered, table)
    gathered = exchange(stat, GROUP)
    moment_two, project, cpad, vector, column, stat = call(
        project_kernel,
        [
            MAP_BLOCK,
            peer_block(peers),
            lane_block(TABLE),
            whole((PADDED, C)),
            whole((SIDE, SIDE, C)),
            se_spec,
            se_spec,
            whole((SE_ROWS, LANES)),
            whole((1, PADDED)),
        ],
        [
            moments,
            (whole((ROWS, C)), EDGE),
            (whole((ROWS, C)), EDGE_BF16),
            (whole((8, PADDED)), f32(8, PADDED)),
            (whole((2, SE_ROWS, LANES)), f32(2, SE_ROWS, LANES)),
            (whole((peers, 4, C)), f32(peers, 4, C)),
        ],
        [
            pltpu.VMEM((CHUNKS, ROWS, LANES), BF16),
            pltpu.VMEM((ROWS, PADDED), BF16),
            line,
        ],
        matmul,
    )(depth, gathered, table, wproj, cot, wred, wres, bred, bres)
    gathered = exchange(stat, GROUP)
    hidden, gpp, rows, reduce, stat = call(
        back_project_kernel,
        [
            MAP_BLOCK,
            whole((peers, 4, C)),
            lane_block(TABLE),
            lane_block(8),
            whole((ROWS, C)),
            whole((ROWS, C)),
            whole((1, C)),
            w_spec,
            whole((8, PADDED)),
            whole((2, SE_ROWS, LANES)),
            se_spec,
            se_spec,
        ],
        [
            (MAP_BLOCK, MAP_BF16),
            (whole((ROWS, C)), EDGE_BF16),
            (whole((8, PADDED)), f32(8, PADDED)),
            (whole((SE_ROWS, LANES)), f32(SE_ROWS, LANES)),
            stat_whole,
        ],
        [map_f32, pltpu.VMEM((8, PADDED), F32)],
        2 * matmul,
    )(
        depth,
        gathered,
        table,
        moment_two,
        project,
        cpad,
        gain_project[None],
        wproj_turn,
        vector,
        column,
        wred,
        wres,
    )
    gathered = exchange(stat, GROUP)
    (early,) = call(
        early_kernel,
        [
            whole((ROWS, C)),
            MAP_BLOCK,
            lane_block(8),
            whole((SE_ROWS, LANES)),
            lane_block(8),
            whole((2, SE_ROWS, LANES)),
            whole((UPPER_ROWS, LANES)),
        ],
        [(whole((EARLY_ROWS, LANES)), f32(EARLY_ROWS, LANES))],
        [],
        10 * matmul,
    )(gpp, hidden, rows, reduce, vector, column, upper_grads[0].reshape(-1, LANES))
    early, gathered = tie(pair_sum(early), gathered)
    early = plane_sum(early)
    grad_one, stat, sums, field, back = call(
        back_depth_kernel,
        [
            MAP_BLOCK,
            xpad_spec,
            w_spec,
            peer_block(peers),
            lane_block(TABLE),
            lane_block(8),
            lane_block(8),
            lane_block(8),
            lane_block(8),
            xpad_spec,
            w_spec,
        ],
        [
            (MAP_BLOCK, MAP),
            stat_out,
            (lane_block(8), f32(8, PADDED)),
            (MAP_BLOCK, MAP_BF16),
            (MAP_BLOCK, MAP_BF16),
        ],
        [map_f32, halo, map_f32, taps, map_f32],
        100 * ROWS * PADDED,
        STREAMED,
    )(
        depth,
        gpp,
        wproj_turn,
        gathered,
        table,
        moment_two,
        moment_one,
        vector,
        rows,
        xpad,
        wexp,
    )
    stat, early, field = lax.optimization_barrier((stat, early, field))
    gathered = exchange(stat, GROUP)
    (sums,) = call(
        kernel_grad_kernel,
        [MAP_BLOCK, MAP_BLOCK, lane_block(8)],
        [(lane_block(TABLE), f32(TABLE, PADDED))],
        [halo],
        50 * ROWS * PADDED,
        STREAMED,
    )(field, back, sums)
    input_grad, late = call(
        back_expand_kernel,
        [
            MAP_BLOCK,
            peer_block(peers),
            lane_block(TABLE),
            lane_block(8),
            xpad_spec,
            w_spec,
            lane_block(TABLE),
            xpad_spec,
            whole((C, ROWS)),
            whole((PADDED, C)),
        ],
        [
            (whole((SIDE, SIDE, C)), jax.ShapeDtypeStruct((SIDE, SIDE, C), BF16)),
            (whole((LATE_ROWS, LANES)), f32(LATE_ROWS, LANES)),
        ],
        [map_f32, pltpu.VMEM((ROWS, PADDED), BF16), pltpu.VMEM((ROWS, C), F32)],
        3 * matmul,
    )(grad_one, gathered, table, moment_one, xpad, wexp, sums, cpad, xpad.T, wexp_turn)

    late = plane_sum(pair_sum(late))
    split = early.shape[0]
    full = all_parts(jnp.concatenate([early, late]))
    early = full[:, :, :split].reshape(EARLY_ROWS, LANES)
    late = full[:, :, split:].reshape(LATE_ROWS, LANES)

    scale = 1.0 / images_total
    wide = (HID,)
    g_project, g_restore, g_reduce, g_brestore, g_shift_two, g_gain_two, g_gproject, g_breduce, upper = (
        unpack(
            unpack_early_kernel,
            early,
            [(C, HID), (SE, HID), (SE, HID), wide, wide, wide, (C,), (SE,), (UPPER_ROWS, LANES)],
            scale,
        )
    )
    g_expand, g_depth, g_shift_one, g_gain_one = unpack(
        unpack_late_kernel, late, [(C, HID), (KER * KER, HID), wide, wide], scale
    )
    return (
        input_grad[None, None],
        g_expand,
        g_gain_one,
        g_shift_one,
        g_depth,
        g_gain_two,
        g_shift_two,
        g_reduce.T,
        g_breduce,
        g_restore,
        g_brestore,
        g_project.T,
        g_gproject,
        upper.reshape(-1),
    )


def solution(mesh):
    chips = Mesh(mesh.devices.reshape(SHAPE), AXES)
    maps = P(("z", "core"), GROUP, None, None, None)
    return jax.shard_map(
        per_device,
        mesh=chips,
        in_specs=(maps, maps) + (P(),) * 12 + (P(AXES, None),),
        out_specs=(maps,) + (P(),) * 13,
        check_vma=False,
    )
```

```python
import functools

import jax
import jax.numpy as jnp
from jax import lax
from jax.experimental import pallas as pl
from jax.experimental.pallas import tpu as pltpu
from jax.sharding import Mesh, PartitionSpec as P

KER = 5
EPSILON = 0.001
SHAPE = (4, 8, 8, 2)
AXES = ("x", "y", "z", "core")
GROUP = ("x", "y")
PLANE = ("y", "z")
SIDE = 29
WIDE = 32
ROWS = SIDE * WIDE
HALO = (SIDE + KER - 1) * WIDE
C = 176
HID = 1056
LANES = 128
CHUNKS = 9
PADDED = CHUNKS * LANES
SE = 44
SE_ROWS = 48
SPOTS = SIDE * SIDE
GAIN_ONE, SHIFT_ONE, GAIN_TWO, SHIFT_TWO, BIAS = 25, 26, 27, 28, 29
TABLE = 32
EARLY = C + 2 * SE_ROWS
UPPER_AT = CHUNKS * EARLY
UPPER_ROWS = 1024
EARLY_ROWS = 3584
LATE = C + TABLE
LATE_ROWS = 2048
PIECE = 4
BATCH = 4
RESIDENT = 20 * 2**20
STREAMED = 56 * 2**20
F32 = jnp.float32
BF16 = jnp.bfloat16


def dot(left, right, left_dim=1, right_dim=0):
    return lax.dot_general(
        left, right, (((left_dim,), (right_dim,)), ((), ())), preferred_element_type=F32
    )


def logistic(values):
    return 0.5 + 0.5 * jnp.tanh(0.5 * values)


def valid_mask(lanes=LANES):
    return lax.broadcasted_iota(jnp.int32, (WIDE, lanes), 0) < SIDE


def row_at(index):
    if isinstance(index, int):
        return slice(index * WIDE, (index + 1) * WIDE)
    return pl.ds(pl.multiple_of(index * WIDE, WIDE), WIDE)


def each_row(body, init):
    for i in range(SIDE):
        init = body(i, init)
    return init


def loop_rows(body, init):
    def several(k, carry):
        for j in range(BATCH):
            carry = body(k * BATCH + j, carry)
        return carry

    init = lax.fori_loop(0, SIDE // BATCH, several, init)
    for i in range(SIDE // BATCH * BATCH, SIDE):
        init = body(i, init)
    return init


def col_sum(values):
    return jnp.sum(values, axis=0, keepdims=True)


def zeros(lanes=LANES):
    return jnp.zeros((WIDE, lanes), F32)


def share(pair, ref):
    ref[...] = jnp.broadcast_to(pair[None], ref.shape)


def pair_rows(first, second):
    return jnp.where(lax.broadcasted_iota(jnp.int32, (2, first.shape[1]), 0) == 0, first, second)


def spread_of(ref, mean, mask):
    def body(i, acc):
        dev = jnp.where(mask, ref[row_at(i), :] - mean, 0.0)
        return acc + dev * dev

    return col_sum(each_row(body, zeros(mean.shape[1]))) / SPOTS


def merged(gathered):
    peers = gathered.shape[0]
    total = jnp.sum(gathered, axis=0)
    center = total[0:1] / peers
    dev = jnp.sum(jnp.square(gathered[:, 0:1, :] - center[None]), axis=0)
    spread = (total[1:2] + dev) / peers
    return center, lax.rsqrt(spread + EPSILON)


def widen(map_ref, flat_ref, line_ref):
    line_ref[...] = jnp.zeros_like(line_ref)
    for i in range(SIDE):
        line_ref[i % 2, 0:SIDE, :] = map_ref[i].astype(F32)
        flat_ref[i * WIDE : (i + 1) * WIDE, :] = line_ref[i % 2].astype(BF16)


def stats_kernel(x_ref, w_ref, xpad_ref, stat_ref, pre_ref, line_ref):
    @pl.when(pl.program_id(0) == 0)
    def _():
        widen(x_ref, xpad_ref, line_ref)

    pre_ref[...] = dot(xpad_ref[...], w_ref[...])
    total = each_row(lambda i, acc: acc + pre_ref[row_at(i), :], zeros())
    mean = col_sum(total) / SPOTS
    share(pair_rows(mean, spread_of(pre_ref, mean, valid_mask())), stat_ref)


def slide(parts, sign):
    out = parts[2]
    for b in (0, 1, 3, 4):
        out = out + pltpu.roll(parts[b], (sign * (2 - b)) % WIDE, 0)
    return out


def row_taps(halo_ref, tap_ref, i, flip):
    parts = [None] * KER
    for a in range(KER):
        source = halo_ref[row_at(i + a), :].reshape(WIDE // 8, 8, LANES)
        for b in range(KER):
            k = ((KER - 1 - a) if flip else a) * KER + b
            term = source * tap_ref[k * 8 : k * 8 + 8, :]
            parts[b] = term if parts[b] is None else parts[b] + term
    return slide([part.reshape(WIDE, LANES) for part in parts], -1 if flip else 1)


def clear_halo(ref):
    edge = jnp.zeros((2 * WIDE, LANES), F32)
    ref[0 : 2 * WIDE, :] = edge
    ref[HALO - 2 * WIDE : HALO, :] = edge


def spread_taps(table_ref, tap_ref):
    for k in range(KER * KER):
        tap_ref[k * 8 : k * 8 + 8, :] = jnp.broadcast_to(table_ref[k : k + 1, :], (8, LANES))


def forward_kernel(
    xpad_ref,
    w_ref,
    gathered_ref,
    table_ref,
    depth_ref,
    stat_ref,
    moment_ref,
    pre_ref,
    halo_ref,
    tap_ref,
):
    @pl.when(pl.program_id(0) == 0)
    def _():
        clear_halo(halo_ref)

    mask = valid_mask()
    center, scale = merged(gathered_ref[...])
    moment_ref[0:1, :] = center
    moment_ref[1:2, :] = scale
    slope = scale * table_ref[GAIN_ONE : GAIN_ONE + 1, :]
    offset = table_ref[SHIFT_ONE : SHIFT_ONE + 1, :] - center * slope
    pre_ref[...] = dot(xpad_ref[...], w_ref[...])

    def activate(i, _):
        act = pre_ref[row_at(i), :] * slope + offset
        silu = (act * logistic(act)).astype(BF16).astype(F32)
        halo_ref[row_at(i + 2), :] = jnp.where(mask, silu, 0.0)
        return 0

    each_row(activate, 0)
    spread_taps(table_ref, tap_ref)

    def filter_row(i, acc):
        out = jnp.where(mask, row_taps(halo_ref, tap_ref, i, False), 0.0)
        depth_ref[row_at(i), :] = out
        return acc + out

    mean = col_sum(loop_rows(filter_row, zeros())) / SPOTS
    share(pair_rows(mean, spread_of(depth_ref, mean, mask)), stat_ref)


def lanes_at(index):
    return pl.ds(pl.multiple_of(index * LANES, LANES), LANES)


def project_kernel(
    depth_ref,
    gathered_ref,
    table_ref,
    wproject_ref,
    cot_ref,
    wreduce_ref,
    wrestore_ref,
    breduce_ref,
    brestore_ref,
    moment_ref,
    project_ref,
    cpad_ref,
    vector_ref,
    column_ref,
    stat_ref,
    act_ref,
    hidden_ref,
    line_ref,
):
    step = pl.program_id(0)
    mask = valid_mask()
    center, scale = merged(gathered_ref[...])
    moment_ref[0:1, :] = center
    moment_ref[1:2, :] = scale
    slope = scale * table_ref[GAIN_TWO : GAIN_TWO + 1, :]
    offset = table_ref[SHIFT_TWO : SHIFT_TWO + 1, :] - center * slope

    def activate(i, acc):
        act = depth_ref[row_at(i), :] * slope + offset
        silu = jnp.where(mask, act * logistic(act), 0.0).astype(BF16)
        act_ref[step, row_at(i), :] = silu
        return acc + silu.astype(F32)

    vector_ref[0:1, lanes_at(step)] = col_sum(each_row(activate, zeros())) / SPOTS

    @pl.when(step == 0)
    def _():
        widen(cot_ref, cpad_ref, line_ref)

    @pl.when(step == CHUNKS - 1)
    def _():
        pooled = vector_ref[0:1, :]
        logit = jnp.sum(wreduce_ref[...] * pooled, axis=1, keepdims=True) + breduce_ref[...]
        squeezed = logit * logistic(logit)
        column_ref[0] = logit
        column_ref[1] = squeezed
        restored = col_sum(wrestore_ref[...] * squeezed[:, 0:1]) + brestore_ref[...]
        vector_ref[1:2, :] = logistic(restored)

        def fill(c, _):
            excite = vector_ref[1:2, lanes_at(c)]

            def scale_row(i, _):
                hidden_ref[row_at(i), lanes_at(c)] = (
                    act_ref[c, row_at(i), :].astype(F32) * excite
                ).astype(BF16)
                return 0

            each_row(scale_row, 0)
            return 0

        lax.fori_loop(0, CHUNKS, fill, 0)
        project_ref[...] = dot(hidden_ref[...], wproject_ref[...])

        def sums(i, accs):
            values, incoming = project_ref[row_at(i), :], cpad_ref[row_at(i), :].astype(F32)
            return accs[0] + values, accs[1] + incoming

        total, cot_total = each_row(sums, (zeros(C), zeros(C)))
        mean = col_sum(total) / SPOTS

        def devs(i, accs):
            dev = jnp.where(valid_mask(C), project_ref[row_at(i), :] - mean, 0.0)
            incoming = cpad_ref[row_at(i), :].astype(F32)
            return accs[0] + dev * dev, accs[1] + incoming * dev

        square, cross = each_row(devs, (zeros(C), zeros(C)))
        row = lax.broadcasted_iota(jnp.int32, (4, C), 0)
        packed = jnp.where(
            row == 0,
            mean,
            jnp.where(
                row == 1,
                col_sum(square) / SPOTS,
                jnp.where(row == 2, col_sum(cot_total), col_sum(cross)),
            ),
        )
        share(packed, stat_ref)


def back_project_kernel(
    depth_ref,
    gathered_ref,
    table_ref,
    moment_ref,
    project_ref,
    cpad_ref,
    gain_ref,
    wproject_ref,
    vector_ref,
    column_ref,
    wreduce_ref,
    wrestore_ref,
    hidden_ref,
    gpp_ref,
    row_ref,
    reduce_ref,
    stat_ref,
    back_ref,
    sums_ref,
):
    step = pl.program_id(0)
    mask = valid_mask()

    @pl.when(step == 0)
    def _():
        gathered = gathered_ref[...]
        peers = gathered.shape[0]
        count = peers * SPOTS
        total = jnp.sum(gathered, axis=0)
        center3 = total[0:1] / peers
        away = gathered[:, 0:1, :] - center3[None]
        spread = (total[1:2] + jnp.sum(jnp.square(away), axis=0)) / peers
        scale3 = lax.rsqrt(spread + EPSILON)
        cross = total[3:4] + jnp.sum(gathered[:, 2:3, :] * away, axis=0)
        first = total[2:3] / count
        second = cross * scale3 / count
        factor = scale3 * gain_ref[...]
        wide = valid_mask(C)

        def body(i, acc):
            normed = (project_ref[row_at(i), :] - center3) * scale3
            incoming = cpad_ref[row_at(i), :].astype(F32)
            grad = factor * (incoming - first - normed * second)
            gpp_ref[row_at(i), :] = jnp.where(wide, grad, 0.0).astype(BF16)
            return acc + incoming * normed

        row_ref[...] = jnp.zeros_like(row_ref)
        row_ref[4:5, 0:C] = col_sum(each_row(body, zeros(C)))

    center, scale = moment_ref[0:1, :], moment_ref[1:2, :]
    gain = table_ref[GAIN_TWO : GAIN_TWO + 1, :]
    shift = table_ref[SHIFT_TWO : SHIFT_TWO + 1, :]
    excite = vector_ref[1:2, lanes_at(step)]
    back_ref[...] = dot(gpp_ref[...], wproject_ref[...])

    def body(i, accs):
        normed = (depth_ref[row_at(i), :] - center) * scale
        act = normed * gain + shift
        sig = logistic(act)
        silu = (act * sig).astype(BF16).astype(F32)
        slope = jnp.where(mask, sig * (1.0 + act * (1.0 - sig)), 0.0)
        hidden_ref[row_at(i), :] = jnp.where(mask, silu * excite, 0.0).astype(BF16)
        back = back_ref[row_at(i), :]
        first = back * slope
        return (
            accs[0] + back * silu,
            accs[1] + first,
            accs[2] + first * normed,
            accs[3] + slope,
            accs[4] + slope * normed,
        )

    totals = each_row(body, tuple(zeros() for _ in range(5)))
    for k in range(5):
        sums_ref[k : k + 1, lanes_at(step)] = col_sum(totals[k])

    @pl.when(step == CHUNKS - 1)
    def _():
        excite = vector_ref[1:2, :]
        logit = column_ref[0]
        grad_logit = sums_ref[0:1, :] * excite * (1.0 - excite)
        grad_squeezed = jnp.sum(wrestore_ref[...] * grad_logit, axis=1, keepdims=True)
        sig = logistic(logit)
        grad_reduce = grad_squeezed * (sig * (1.0 + logit * (1.0 - sig)))
        grad_pooled = col_sum(wreduce_ref[...] * grad_reduce[:, 0:1]) / SPOTS
        shift_sum = excite * sums_ref[1:2, :] + grad_pooled * sums_ref[3:4, :]
        gain_sum = excite * sums_ref[2:3, :] + grad_pooled * sums_ref[4:5, :]
        share(pair_rows(shift_sum, gain_sum), stat_ref)
        row_ref[0:1, :] = grad_pooled
        row_ref[1:2, :] = grad_logit
        row_ref[2:3, :] = shift_sum
        row_ref[3:4, :] = gain_sum
        reduce_ref[...] = grad_reduce


def early_kernel(
    gpp_ref, hidden_ref, row_ref, reduce_ref, vector_ref, column_ref, upper_ref, grads_ref
):
    step = pl.program_id(0)
    base = pl.multiple_of(step * EARLY, 16)
    grads_ref[pl.ds(base, C), :] = dot(gpp_ref[...], hidden_ref[...], 0, 0)
    lane = lax.broadcasted_iota(jnp.int32, (SE_ROWS, LANES), 1)
    row = lax.broadcasted_iota(jnp.int32, (SE_ROWS, LANES), 0)
    squeezed, grad_reduce = column_ref[1], reduce_ref[...]
    block = squeezed * row_ref[1:2, :]
    block = jnp.where(row == SE, row_ref[1:2, :], block)
    block = jnp.where(row == SE + 1, row_ref[2:3, :], block)
    block = jnp.where(row == SE + 2, row_ref[3:4, :], block)
    bias_row = col_sum(jnp.where(lane == row, grad_reduce, 0.0))
    extra = jnp.where(step < 2, row_ref[4:5, :], bias_row)
    block = jnp.where(row == SE + 3, extra, block)
    grads_ref[pl.ds(pl.multiple_of(base + C, 16), SE_ROWS), :] = block
    grads_ref[pl.ds(pl.multiple_of(base + C + SE_ROWS, 16), SE_ROWS), :] = (
        grad_reduce * vector_ref[0:1, :]
    )

    @pl.when(step == 0)
    def _():
        grads_ref[UPPER_AT : UPPER_AT + UPPER_ROWS, :] = upper_ref[...]
        rest = EARLY_ROWS - UPPER_AT - UPPER_ROWS
        grads_ref[UPPER_AT + UPPER_ROWS :, :] = jnp.zeros((rest, LANES), F32)


def back_depth_kernel(
    depth_ref,
    gpp_ref,
    wproject_ref,
    gathered_ref,
    table_ref,
    moment_two_ref,
    moment_one_ref,
    vector_ref,
    pooled_ref,
    xpad_ref,
    w_ref,
    grad_ref,
    stat_ref,
    sums_ref,
    field_ref,
    back_ref,
    pre_ref,
    ghalo_ref,
    side_ref,
    tap_ref,
    product_ref,
):
    @pl.when(pl.program_id(0) == 0)
    def _():
        clear_halo(ghalo_ref)

    mask = valid_mask()
    total = jnp.sum(gathered_ref[...], axis=0)
    gain = table_ref[GAIN_TWO : GAIN_TWO + 1, :]
    count = gathered_ref.shape[0] * SPOTS
    mean_first = gain * total[0:1] / count
    mean_second = gain * total[1:2] / count
    center, scale = moment_two_ref[0:1, :], moment_two_ref[1:2, :]
    shift = table_ref[SHIFT_TWO : SHIFT_TWO + 1, :]
    excite = vector_ref[1:2, :] * gain
    pooled = pooled_ref[0:1, :] * gain
    product_ref[...] = dot(gpp_ref[...], wproject_ref[...])
    center_one, scale_one = moment_one_ref[0:1, :], moment_one_ref[1:2, :]
    slope_one = scale_one * table_ref[GAIN_ONE : GAIN_ONE + 1, :]
    offset_one = table_ref[SHIFT_ONE : SHIFT_ONE + 1, :] - center_one * slope_one
    pre_ref[...] = dot(xpad_ref[...], w_ref[...])

    def prepare(i, _):
        normed = (depth_ref[row_at(i), :] - center) * scale
        act = normed * gain + shift
        sig = logistic(act)
        grad = (product_ref[row_at(i), :] * excite + pooled) * (sig * (1.0 + act * (1.0 - sig)))
        grad = jnp.where(mask, scale * (grad - mean_first - normed * mean_second), 0.0)
        ghalo_ref[row_at(i + 2), :] = grad
        back_ref[row_at(i), :] = grad.astype(BF16)
        act = pre_ref[row_at(i), :] * slope_one + offset_one
        sig = logistic(act)
        field_ref[row_at(i), :] = jnp.where(mask, act * sig, 0.0).astype(BF16)
        side_ref[row_at(i), :] = jnp.where(mask, sig * (1.0 + act * (1.0 - sig)), 0.0)
        return 0

    each_row(prepare, 0)
    spread_taps(table_ref, tap_ref)

    def input_grad(i, accs):
        grad = row_taps(ghalo_ref, tap_ref, i, True) * side_ref[row_at(i), :]
        grad_ref[row_at(i), :] = grad
        normed = (pre_ref[row_at(i), :] - center_one) * scale_one
        return accs[0] + grad, accs[1] + grad * normed

    shift_sum, gain_sum = (col_sum(a) for a in loop_rows(input_grad, (zeros(), zeros())))
    share(pair_rows(shift_sum, gain_sum), stat_ref)
    sums_ref[...] = jnp.zeros_like(sums_ref)
    sums_ref[0:1, :] = shift_sum
    sums_ref[1:2, :] = gain_sum


def kernel_grad_kernel(field_ref, back_ref, sums_ref, out_ref, halo_ref):
    @pl.when(pl.program_id(0) == 0)
    def _():
        clear_halo(halo_ref)

    halo_ref[2 * WIDE : 2 * WIDE + ROWS, :] = field_ref[...].astype(F32)

    def kernel_grad(i, accs):
        grad = back_ref[row_at(i), :].astype(F32)
        shifted = [
            (grad if b == 2 else pltpu.roll(grad, (b - 2) % WIDE, 0)).reshape(
                WIDE // 8, 8, LANES
            )
            for b in range(KER)
        ]
        accs = list(accs)
        for a in range(KER):
            field = halo_ref[row_at(i + a), :].reshape(WIDE // 8, 8, LANES)
            for b in range(KER):
                accs[a * KER + b] = accs[a * KER + b] + jnp.sum(field * shifted[b], axis=0)
        return tuple(accs)

    start = tuple(jnp.zeros((8, LANES), F32) for _ in range(KER * KER))
    accs = loop_rows(kernel_grad, start)
    for k in range(KER * KER):
        out_ref[k : k + 1, :] = col_sum(accs[k])
    out_ref[25:TABLE, :] = sums_ref[0 : TABLE - 25, :]


def back_expand_kernel(
    grad_ref,
    gathered_ref,
    table_ref,
    moment_ref,
    xpad_ref,
    w_ref,
    sums_ref,
    cpad_ref,
    xturn_ref,
    wturn_ref,
    out_ref,
    grads_ref,
    pre_ref,
    gpe_ref,
    acc_ref,
):
    step = pl.program_id(0)
    mask = valid_mask()
    total = jnp.sum(gathered_ref[...], axis=0)
    count = gathered_ref.shape[0] * SPOTS
    mean_first, mean_second = total[0:1] / count, total[1:2] / count
    center, scale = moment_ref[0:1, :], moment_ref[1:2, :]
    factor = scale * table_ref[GAIN_ONE : GAIN_ONE + 1, :]
    pre_ref[...] = dot(xpad_ref[...], w_ref[...])

    def body(i, _):
        normed = (pre_ref[row_at(i), :] - center) * scale
        grad = factor * (grad_ref[row_at(i), :] - mean_first - normed * mean_second)
        gpe_ref[row_at(i), lanes_at(step)] = jnp.where(mask, grad, 0.0).astype(BF16)
        return 0

    each_row(body, 0)
    base = pl.multiple_of(step * LATE, 16)
    grads_ref[pl.ds(base, C), :] = dot(xturn_ref[...], gpe_ref[:, lanes_at(step)])
    grads_ref[pl.ds(pl.multiple_of(base + C, 16), TABLE), :] = sums_ref[...]

    @pl.when(step == CHUNKS - 1)
    def _():
        grads_ref[CHUNKS * LATE :, :] = jnp.zeros((LATE_ROWS - CHUNKS * LATE, LANES), F32)
        acc_ref[...] = cpad_ref[...].astype(F32) + dot(gpe_ref[...], wturn_ref[...])
        for i in range(SIDE):
            out_ref[i] = acc_ref[i * WIDE : i * WIDE + SIDE, :].astype(BF16)


def put_row(ref, rows_ref, row, height, scale):
    for c in range(-(-ref.shape[-1] // LANES)):
        width = min(LANES, ref.shape[-1] - c * LANES)
        at = c * height + row
        if len(ref.shape) == 1:
            ref[c * LANES : c * LANES + width] = rows_ref[at, 0:width] * scale
            continue
        ref[:, c * LANES : c * LANES + width] = rows_ref[at : at + ref.shape[0], 0:width] * scale


def unpack_early_kernel(
    scale,
    rows_ref,
    project_ref,
    restore_ref,
    reduce_ref,
    brestore_ref,
    shift_ref,
    gain_ref,
    gproject_ref,
    breduce_ref,
    upper_ref,
):
    put_row(project_ref, rows_ref, 0, EARLY, scale)
    put_row(restore_ref, rows_ref, C, EARLY, scale)
    put_row(reduce_ref, rows_ref, C + SE_ROWS, EARLY, scale)
    put_row(brestore_ref, rows_ref, C + SE, EARLY, scale)
    put_row(shift_ref, rows_ref, C + SE + 1, EARLY, scale)
    put_row(gain_ref, rows_ref, C + SE + 2, EARLY, scale)
    put_row(gproject_ref, rows_ref, C + SE + 3, EARLY, scale)
    at = 2 * EARLY + C + SE + 3
    breduce_ref[...] = rows_ref[at, 0:SE] * scale
    upper_ref[...] = rows_ref[UPPER_AT : UPPER_AT + UPPER_ROWS, :]


def unpack_late_kernel(scale, rows_ref, expand_ref, depth_ref, shift_ref, gain_ref):
    put_row(expand_ref, rows_ref, 0, LATE, scale)
    put_row(depth_ref, rows_ref, C, LATE, scale)
    put_row(shift_ref, rows_ref, C + 25, LATE, scale)
    put_row(gain_ref, rows_ref, C + 26, LATE, scale)


def unpack(kernel, rows, shapes, scale):
    return pl.pallas_call(
        functools.partial(kernel, scale),
        out_shape=tuple(f32(*shape) for shape in shapes),
        compiler_params=pltpu.CompilerParams(vmem_limit_bytes=RESIDENT),
        cost_estimate=pl.CostEstimate(
            flops=rows.size, bytes_accessed=8 * rows.size, transcendentals=0
        ),
    )(rows)


def whole(shape):
    return pl.BlockSpec(shape, lambda c: (0,) * len(shape))


def lane_block(rows):
    return pl.BlockSpec((rows, LANES), lambda c: (0, c))


def peer_block(peers):
    return pl.BlockSpec((peers, 2, LANES), lambda c: (0, 0, c))


MAP_BLOCK = pl.BlockSpec((pl.squeezed, ROWS, LANES), lambda c: (c, 0, 0))
MAP = jax.ShapeDtypeStruct((CHUNKS, ROWS, LANES), F32)
MAP_BF16 = jax.ShapeDtypeStruct((CHUNKS, ROWS, LANES), BF16)
EDGE = jax.ShapeDtypeStruct((ROWS, C), F32)
EDGE_BF16 = jax.ShapeDtypeStruct((ROWS, C), BF16)


def f32(*shape):
    return jax.ShapeDtypeStruct(shape, F32)


def call(kernel, ins, outs, scratch, flops, vmem=RESIDENT):
    return pl.pallas_call(
        kernel,
        grid=(CHUNKS,),
        in_specs=ins,
        out_specs=tuple(spec for spec, _ in outs),
        out_shape=tuple(shape for _, shape in outs),
        scratch_shapes=scratch,
        compiler_params=pltpu.CompilerParams(vmem_limit_bytes=vmem),
        cost_estimate=pl.CostEstimate(
            flops=flops, bytes_accessed=12 * 2**20, transcendentals=ROWS * PADDED
        ),
    )


def exchange(copies, axes):
    return lax.all_to_all(copies, axes, 0, 0, tiled=True)


def swap(rows):
    return lax.ppermute(rows, "core", [(i, i ^ 1) for i in range(lax.axis_size("core"))])


def pair_sum(rows):
    plane = lax.axis_size(PLANE)
    near = lax.axis_index("core") == 0
    halves = rows.reshape(2, plane, -1, PIECE, LANES)
    mine = jnp.where(near, halves[0], halves[1])
    return mine + swap(jnp.where(near, halves[1], halves[0]))


def plane_sum(mine):
    return jnp.sum(exchange(mine, PLANE), axis=0)


def all_parts(mine):
    plane, line = lax.axis_size(PLANE), lax.axis_size("x")
    near = lax.axis_index("core") == 0
    mine = jnp.sum(exchange(jnp.broadcast_to(mine[None], (line,) + mine.shape), "x"), axis=0)
    half = exchange(jnp.broadcast_to(mine[None], (plane,) + mine.shape), PLANE)
    other = swap(half)
    return jnp.stack([jnp.where(near, half, other), jnp.where(near, other, half)])


def tie(first, second):
    return lax.optimization_barrier((first, second))


def per_device(
    block_input,
    cotangent,
    w_expand,
    gain_expand,
    shift_expand,
    w_depth,
    gain_depth,
    shift_depth,
    w_reduce,
    b_reduce,
    w_restore,
    b_restore,
    w_project,
    gain_project,
    upper_grads,
):
    peers = lax.axis_size(GROUP)
    images_total = lax.axis_size(AXES)
    extra = PADDED - HID
    images, cot = block_input[0, 0], cotangent[0, 0]
    wexp = jnp.pad(w_expand, ((0, 0), (0, extra)))
    wproj = jnp.pad(w_project, ((0, extra), (0, 0)))
    wproj_turn = jnp.pad(w_project.T, ((0, 0), (0, extra)))
    wexp_turn = jnp.pad(w_expand.T, ((0, extra), (0, 0)))
    wred = jnp.pad(w_reduce.astype(F32).T, ((0, SE_ROWS - SE), (0, extra)))
    wres = jnp.pad(w_restore.astype(F32), ((0, SE_ROWS - SE), (0, extra)))
    bred = jnp.broadcast_to(jnp.pad(b_reduce, (0, SE_ROWS - SE))[:, None], (SE_ROWS, LANES))
    bres = jnp.pad(b_restore, (0, extra))[None]
    table = jnp.concatenate(
        [w_depth.astype(F32)]
        + [v[None] for v in (gain_expand, shift_expand, gain_depth, shift_depth)],
        axis=0,
    )
    table = jnp.pad(table, ((0, TABLE - table.shape[0]), (0, extra)))
    xpad_spec, w_spec = whole((ROWS, C)), lane_block(C)
    se_spec = whole((SE_ROWS, PADDED))
    stat_out = (peer_block(peers), f32(peers, 2, PADDED))
    stat_whole = (whole((peers, 2, PADDED)), f32(peers, 2, PADDED))
    moments = (lane_block(8), f32(8, PADDED))
    map_f32 = pltpu.VMEM((ROWS, LANES), F32)
    map_bf16 = pltpu.VMEM((ROWS, LANES), BF16)
    line = pltpu.VMEM((2, WIDE, C), F32)
    taps = pltpu.VMEM((KER * KER * 8, LANES), F32)
    halo = pltpu.VMEM((HALO, LANES), F32)
    matmul = 2 * ROWS * C * PADDED

    xpad, stat = call(
        stats_kernel,
        [whole((SIDE, SIDE, C)), w_spec],
        [(xpad_spec, EDGE_BF16), stat_out],
        [map_f32, line],
        matmul,
    )(images, wexp)
    gathered = exchange(stat, GROUP)
    depth, stat, moment_one = call(
        forward_kernel,
        [xpad_spec, w_spec, peer_block(peers), lane_block(TABLE)],
        [(MAP_BLOCK, MAP), stat_out, moments],
        [map_f32, halo, taps],
        50 * ROWS * PADDED,
        STREAMED,
    )(xpad, wexp, gathered, table)
    gathered = exchange(stat, GROUP)
    moment_two, project, cpad, vector, column, stat = call(
        project_kernel,
        [
            MAP_BLOCK,
            peer_block(peers),
            lane_block(TABLE),
            whole((PADDED, C)),
            whole((SIDE, SIDE, C)),
            se_spec,
            se_spec,
            whole((SE_ROWS, LANES)),
            whole((1, PADDED)),
        ],
        [
            moments,
            (whole((ROWS, C)), EDGE),
            (whole((ROWS, C)), EDGE_BF16),
            (whole((8, PADDED)), f32(8, PADDED)),
            (whole((2, SE_ROWS, LANES)), f32(2, SE_ROWS, LANES)),
            (whole((peers, 4, C)), f32(peers, 4, C)),
        ],
        [
            pltpu.VMEM((CHUNKS, ROWS, LANES), BF16),
            pltpu.VMEM((ROWS, PADDED), BF16),
            line,
        ],
        matmul,
    )(depth, gathered, table, wproj, cot, wred, wres, bred, bres)
    gathered = exchange(stat, GROUP)
    hidden, gpp, rows, reduce, stat = call(
        back_project_kernel,
        [
            MAP_BLOCK,
            whole((peers, 4, C)),
            lane_block(TABLE),
            lane_block(8),
            whole((ROWS, C)),
            whole((ROWS, C)),
            whole((1, C)),
            w_spec,
            whole((8, PADDED)),
            whole((2, SE_ROWS, LANES)),
            se_spec,
            se_spec,
        ],
        [
            (MAP_BLOCK, MAP_BF16),
            (whole((ROWS, C)), EDGE_BF16),
            (whole((8, PADDED)), f32(8, PADDED)),
            (whole((SE_ROWS, LANES)), f32(SE_ROWS, LANES)),
            stat_whole,
        ],
        [map_f32, pltpu.VMEM((8, PADDED), F32)],
        2 * matmul,
    )(
        depth,
        gathered,
        table,
        moment_two,
        project,
        cpad,
        gain_project[None],
        wproj_turn,
        vector,
        column,
        wred,
        wres,
    )
    gathered = exchange(stat, GROUP)
    (early,) = call(
        early_kernel,
        [
            whole((ROWS, C)),
            MAP_BLOCK,
            lane_block(8),
            whole((SE_ROWS, LANES)),
            lane_block(8),
            whole((2, SE_ROWS, LANES)),
            whole((UPPER_ROWS, LANES)),
        ],
        [(whole((EARLY_ROWS, LANES)), f32(EARLY_ROWS, LANES))],
        [],
        10 * matmul,
    )(gpp, hidden, rows, reduce, vector, column, upper_grads[0].reshape(-1, LANES))
    early, gathered = tie(pair_sum(early), gathered)
    early = plane_sum(early)
    grad_one, stat, sums, field, back = call(
        back_depth_kernel,
        [
            MAP_BLOCK,
            xpad_spec,
            w_spec,
            peer_block(peers),
            lane_block(TABLE),
            lane_block(8),
            lane_block(8),
            lane_block(8),
            lane_block(8),
            xpad_spec,
            w_spec,
        ],
        [
            (MAP_BLOCK, MAP),
            stat_out,
            (lane_block(8), f32(8, PADDED)),
            (MAP_BLOCK, MAP_BF16),
            (MAP_BLOCK, MAP_BF16),
        ],
        [map_f32, halo, map_f32, taps, map_f32],
        100 * ROWS * PADDED,
        STREAMED,
    )(
        depth,
        gpp,
        wproj_turn,
        gathered,
        table,
        moment_two,
        moment_one,
        vector,
        rows,
        xpad,
        wexp,
    )
    stat, early, field = lax.optimization_barrier((stat, early, field))
    gathered = exchange(stat, GROUP)
    (sums,) = call(
        kernel_grad_kernel,
        [MAP_BLOCK, MAP_BLOCK, lane_block(8)],
        [(lane_block(TABLE), f32(TABLE, PADDED))],
        [halo],
        50 * ROWS * PADDED,
        STREAMED,
    )(field, back, sums)
    input_grad, late = call(
        back_expand_kernel,
        [
            MAP_BLOCK,
            peer_block(peers),
            lane_block(TABLE),
            lane_block(8),
            xpad_spec,
            w_spec,
            lane_block(TABLE),
            xpad_spec,
            whole((C, ROWS)),
            whole((PADDED, C)),
        ],
        [
            (whole((SIDE, SIDE, C)), jax.ShapeDtypeStruct((SIDE, SIDE, C), BF16)),
            (whole((LATE_ROWS, LANES)), f32(LATE_ROWS, LANES)),
        ],
        [map_f32, pltpu.VMEM((ROWS, PADDED), BF16), pltpu.VMEM((ROWS, C), F32)],
        3 * matmul,
    )(grad_one, gathered, table, moment_one, xpad, wexp, sums, cpad, xpad.T, wexp_turn)

    late = plane_sum(pair_sum(late))
    split = early.shape[0]
    full = all_parts(jnp.concatenate([early, late]))
    early = full[:, :, :split].reshape(EARLY_ROWS, LANES)
    late = full[:, :, split:].reshape(LATE_ROWS, LANES)

    scale = 1.0 / images_total
    wide = (HID,)
    g_project, g_restore, g_reduce, g_brestore, g_shift_two, g_gain_two, g_gproject, g_breduce, upper = (
        unpack(
            unpack_early_kernel,
            early,
            [(C, HID), (SE, HID), (SE, HID), wide, wide, wide, (C,), (SE,), (UPPER_ROWS, LANES)],
            scale,
        )
    )
    g_expand, g_depth, g_shift_one, g_gain_one = unpack(
        unpack_late_kernel, late, [(C, HID), (KER * KER, HID), wide, wide], scale
    )
    return (
        input_grad[None, None],
        g_expand,
        g_gain_one,
        g_shift_one,
        g_depth,
        g_gain_two,
        g_shift_two,
        g_reduce.T,
        g_breduce,
        g_restore,
        g_brestore,
        g_project.T,
        g_gproject,
        upper.reshape(-1),
    )


def solution(mesh):
    chips = Mesh(mesh.devices.reshape(SHAPE), AXES)
    maps = P(("z", "core"), GROUP, None, None, None)
    return jax.shard_map(
        per_device,
        mesh=chips,
        in_specs=(maps, maps) + (P(),) * 12 + (P(AXES, None),),
        out_specs=(maps,) + (P(),) * 13,
        check_vma=False,
    )
```
